256 devices in a mesh: expert: 8 (over x, core), dp: 32 (over y, z).
Axes of the slice: x: 4, y: 4, z: 8, core: 2. Of those that a mesh axis runs over, the one named last changes fastest.
Arguments:
- tokens: bfloat16 [32768, 1664], P(('expert', 'dp')), may hold values from -6 to 6
- expert_ids: int32 [32768, 2], P(('expert', 'dp')), may hold values from 0 to 15, as said below
- slot_ids: int32 [32768, 2], P(('expert', 'dp')), may hold values from 0 to 3, as said below
- dropped: int32 [32768, 2], P(('expert', 'dp')), may hold values from 0 to 1, as said below
- gates: float32 [32768, 2], P(('expert', 'dp')), may hold values from 0.1 to 1
- w_in: bfloat16 [16, 1664, 8192], P('expert', None, 'dp'), may hold values from -0.15625 to 0.15625
- w_out: bfloat16 [16, 8192, 1664], P('expert', 'dp'), may hold values from -0.0625 to 0.0625
- out_grad: bfloat16 [32768, 1664], P(('expert', 'dp')), may hold values from -6 to 6
Outputs:
- mixed: bfloat16 [32768, 1664], P(('expert', 'dp'))
- tok_grad: bfloat16 [32768, 1664], P(('expert', 'dp'))
- gate_grad: float32 [32768, 2], P(('expert', 'dp'))
- w_in_grad: float32 [16, 1664, 8192], P('expert', None, 'dp')
- w_out_grad: float32 [16, 8192, 1664], P('expert', 'dp')
The draws below stay inside these ranges and needn't reach their ends.
Inputs may be any that keep to these rules, and one draw needn't show every extreme that they name: `expert_ids`: the two experts of a token differ. `slot_ids`: choices are ranked in each block of 128 tokens by batch priority, all first choices before all second choices; a choice's slot is the number of higher-ranked choices of the same block to the same expert; it is dropped where that number is 4 or more, and its slot is then 0. Kept choices of one expert in one block have distinct slots. In every draw one expert is the first choice of at least 5 tokens of every block. `dropped`: 1 exactly where the slot count described for slot_ids reaches 4.
All inputs are finite; a program needn't handle non-finite values.
Results may differ from the reference program's by a relative error of at most 0.039.
Values may be sent and summed in bfloat16 or wider, within the bound.
A program may use at most 128 MiB of HBM per device.

```python
import jax
import jax.numpy as jnp
from jax import lax

D = 1664
FF = 8192
CAP = 4
TOK_DEV = 128
EXPERTS = 16
TOKENS = 32768
N_DP = 32


def routing(key):
    base = jax.random.fold_in(key, 101)
    blocks = TOKENS // TOK_DEV
    key_hot, key_rank, key_first, key_second = jax.random.split(base, 4)
    favored = jax.random.randint(key_hot, (), 0, EXPERTS)

    def shuffle(sub_key):
        return jax.random.permutation(sub_key, TOK_DEV).astype(jnp.int32)
    priority = jax.vmap(shuffle)(jax.random.split(key_rank, blocks))
    random_first = jax.random.randint(key_first, (blocks, TOK_DEV), 0, EXPERTS)
    first = jnp.where(priority < CAP + 1, favored, random_first).astype(jnp.int32)
    offset = jax.random.randint(key_second, (blocks, TOK_DEV), 0, EXPERTS - 1)
    second = ((first + 1 + offset) % EXPERTS).astype(jnp.int32)
    chosen = jnp.stack([first, second], axis=-1)
    order_key = jnp.stack([priority, priority + TOK_DEV], axis=-1)
    flat_expert = chosen.reshape(blocks, 2 * TOK_DEV)
    flat_order = order_key.reshape(blocks, 2 * TOK_DEV)
    earlier = (flat_order[:, None, :] < flat_order[:, :, None]) & (flat_expert[:, None, :] == flat_expert[:, :, None])
    position = jnp.sum(earlier.astype(jnp.int32), axis=-1)
    overflow = (position >= CAP).astype(jnp.int32)
    slots = jnp.where(overflow > 0, 0, position).astype(jnp.int32)
    return (chosen.reshape(TOKENS, 2), slots.reshape(TOKENS, 2), overflow.reshape(TOKENS, 2))


def draw_expert_ids(key, part):
    return routing(key)[0]


def draw_slot_ids(key, part):
    return routing(key)[1]


def draw_dropped(key, part):
    return routing(key)[2]


def levels(own_key, shape, pieces, low, largest):
    gain = 1.0
    for dim, parts in pieces:
        steps = jax.random.uniform(jax.random.fold_in(jax.random.fold_in(own_key, 6), dim), (parts,), jnp.float32, low / len(pieces), largest / len(pieces))
        gain = gain * jnp.repeat(jnp.exp(steps), shape[dim] // parts).reshape((-1,) + (1,) * (len(shape) - 1 - dim))
    return gain


def noise(own_key, dims, scale, bound, cuts=(), kind=jnp.bfloat16):
    values = jax.random.normal(own_key, dims, jnp.float32) * scale
    if len(cuts) > 0:
        values = levels(own_key, dims, cuts, -0.22, 0.18) * values
    return jnp.clip(values, min=-bound, max=bound).astype(kind)


def setup_inputs(seed: int = 0) -> dict:
    arg_keys = jax.random.split(jax.random.key(seed), 9)
    tokens = noise(arg_keys[0], (TOKENS, D), 1.0, 6.0, ((0, 256),))
    expert_ids = draw_expert_ids(jax.random.fold_in(arg_keys[8], 71), 0)
    slot_ids = draw_slot_ids(jax.random.fold_in(arg_keys[8], 71), 0)
    dropped = draw_dropped(jax.random.fold_in(arg_keys[8], 71), 0)
    gates = jnp.clip(0.1 + 0.9 * jax.random.uniform(arg_keys[4], (TOKENS, 2), jnp.float32) ** levels(arg_keys[4], (TOKENS, 2), ((0, 256),), -0.2, 0.2), 0.1, 1.0)
    w_in = noise(arg_keys[5], (EXPERTS, D, FF), D ** -0.5, 0.15625, ((0, 8), (2, 32)))
    w_out = noise(arg_keys[6], (EXPERTS, FF, D), FF ** -0.5, 0.0625, ((0, 8), (1, 32)))
    out_grad = noise(arg_keys[7], (TOKENS, D), 1.0, 6.0, ((0, 256),))
    return {"tokens": tokens, "expert_ids": expert_ids, "slot_ids": slot_ids, "dropped": dropped, "gates": gates, "w_in": w_in, "w_out": w_out, "out_grad": out_grad}


inv_root_two = 0.7071067811865476
inv_root_two_pi = 0.3989422804014327


def gelu_exact(value):
    return 0.5 * value * (1.0 + lax.erf(value * inv_root_two))


def gelu_slope(value):
    return 0.5 * (1.0 + lax.erf(value * inv_root_two)) + value * jnp.exp(-0.5 * value * value) * inv_root_two_pi


def group_sum(left, right):
    count = left.shape[0]
    width = right.shape[1]
    group = FF // N_DP
    left_parts = left.reshape(count, N_DP, group).transpose(1, 0, 2)
    right_parts = right.reshape(N_DP, group, width)

    def add_group(total, pair):
        term = jnp.dot(pair[0], pair[1], preferred_element_type=jnp.float32).astype(jnp.bfloat16)
        return total + term.astype(jnp.float32), None

    total, unused = lax.scan(add_group, jnp.zeros((count, width), jnp.float32), (left_parts, right_parts))
    return total.astype(jnp.bfloat16)


def expert_pass(packed):
    rows, grad_rows, weight_in, weight_out = packed
    pre = jnp.dot(rows, weight_in, preferred_element_type=jnp.float32)
    hidden = gelu_exact(pre).astype(jnp.bfloat16)
    output = group_sum(hidden, weight_out)
    hidden_grad = jnp.dot(grad_rows, weight_out.T, preferred_element_type=jnp.float32)
    pre_grad = (hidden_grad * gelu_slope(pre)).astype(jnp.bfloat16)
    weight_out_grad = jnp.dot(hidden.T, grad_rows, preferred_element_type=jnp.float32)
    weight_in_grad = jnp.dot(rows.T, pre_grad, preferred_element_type=jnp.float32)
    row_grad = group_sum(pre_grad, weight_in.T)
    return output, row_grad, weight_in_grad, weight_out_grad


def reference(tokens, expert_ids, slot_ids, dropped, gates, w_in, w_out, out_grad):
    blocks = TOKENS // TOK_DEV
    columns = EXPERTS * CAP
    block_of = (jnp.arange(TOKENS, dtype=jnp.int32) // TOK_DEV).astype(jnp.int32)
    target = jnp.where(dropped == 0, expert_ids * CAP + slot_ids, columns).astype(jnp.int32)
    block_idx = jnp.broadcast_to(block_of[:, None], target.shape)
    token_rows = jnp.broadcast_to(tokens[:, None, :], (TOKENS, 2, D))
    buffer = jnp.zeros((blocks, columns + 1, D), jnp.bfloat16).at[block_idx, target].set(token_rows)
    scaled = (gates[:, :, None] * out_grad.astype(jnp.float32)[:, None, :]).astype(jnp.bfloat16)
    grad_buffer = jnp.zeros((blocks, columns + 1, D), jnp.bfloat16).at[block_idx, target].set(scaled)

    def by_expert(array):
        return array[:, :columns].reshape(blocks, EXPERTS, CAP, D).transpose(1, 0, 2, 3).reshape(EXPERTS, blocks * CAP, D)

    def by_block(array):
        back = array.reshape(EXPERTS, blocks, CAP, D).transpose(1, 0, 2, 3).reshape(blocks, columns, D)
        return jnp.concatenate([back, jnp.zeros((blocks, 1, D), back.dtype)], axis=1)

    outputs, row_grads, w_in_grad, w_out_grad = lax.map(expert_pass, (by_expert(buffer), by_expert(grad_buffer), w_in, w_out))
    picked = by_block(outputs)[block_idx, target].astype(jnp.float32)
    mixed = jnp.sum(gates[:, :, None] * picked, axis=1).astype(jnp.bfloat16)
    gate_grad = jnp.sum(picked * out_grad.astype(jnp.float32)[:, None, :], axis=-1)
    picked_grad = by_block(row_grads)[block_idx, target].astype(jnp.float32)
    tok_grad = jnp.sum(picked_grad, axis=1).astype(jnp.bfloat16)
    return mixed, tok_grad, gate_grad, w_in_grad, w_out_grad
```

```python
import jax
import jax.numpy as jnp
from jax import lax
from jax.experimental import pallas as pl
from jax.experimental.pallas import tpu as pltpu
from jax.sharding import PartitionSpec as P

CAP = 4
N_EXP = 8
N_DP = 32
HALF = 16
BF16 = jnp.bfloat16
F32 = jnp.float32
MESH = pl.DeviceIdType.MESH

inv_root_two = 0.7071067811865476
inv_root_two_pi = 0.3989422804014327


def place_first(y, z):
    return 4 * z + (y + z) % 4


def device_first(p):
    z = p // 4
    return ((p % 4 + 8 - z) % 4) * 8 + z


def place_second(y, z):
    w = (z + 24 - 3 * y) % 8
    return 4 * y + 16 * (w // 4) + w % 4


def device_second(p):
    q = p // 4
    return (q % 4) * 8 + (3 * q + p % 4) % 8


def dot(left, right, left_dim, right_dim):
    return lax.dot_general(
        left, right, (((left_dim,), (right_dim,)), ((), ())), preferred_element_type=F32
    )


def kernel(
    tokens, ids, slots, dropped, gates, out_grad, w_in_hbm, w_out_hbm,
    mixed, tok_grad, gate_grad, w_in_grad, w_out_grad,
    gathered, part, arrived, hidden, pre_grad, w_in, w_out, send, recv, back,
    load_sem, a2a_send, a2a_recv, ag_send, ag_recv, rs_send, rs_recv, ret_send, ret_recv,
):
    width = tokens.shape[1]
    me_e = lax.axis_index("expert")
    me_d = lax.axis_index("dp")
    y, z = me_d // 8, me_d % 8
    here = (place_first(y, z), place_second(y, z))
    device = (device_first, device_second)
    near = [[device[c]((here[c] + step) % N_DP) for step in (1, N_DP - 1)] for c in range(2)]

    load_in = pltpu.make_async_copy(w_in_hbm, w_in, load_sem.at[0])
    load_out = pltpu.make_async_copy(w_out_hbm, w_out, load_sem.at[1])
    load_in.start()
    load_out.start()

    barrier = pltpu.get_barrier_semaphore()

    def greet(k, carry):
        pl.semaphore_signal(
            barrier, inc=1, device_id={"expert": (me_e + k) % N_EXP}, device_id_type=MESH
        )
        return carry

    lax.fori_loop(1, N_EXP, greet, 0)
    for c in range(2):
        for d in range(2):
            pl.semaphore_signal(barrier, inc=1, device_id={"dp": near[c][d]}, device_id_type=MESH)

    expert = ids[...]
    column = (expert >> 1) * 16 + (expert & 1) * 4 + slots[...]
    column = jnp.where(dropped[...] == 0, column, -64)
    lane = lax.broadcasted_iota(jnp.int32, (128, 128), 1)
    pick = [column[:, k : k + 1] == lane for k in range(2)]
    pick_grad = [column[:, k : k + 1] + 8 == lane for k in range(2)]

    def onehot(mask):
        return jnp.where(mask, 1.0, 0.0).astype(BF16)

    grad_wide = out_grad[...].astype(F32)
    packed = dot(onehot(pick[0] | pick[1]), tokens[...], 0, 0)
    for k in range(2):
        scaled = (gates[:, k : k + 1] * grad_wide).astype(BF16)
        packed += dot(onehot(pick_grad[k]), scaled, 0, 0)
    send[...] = packed.astype(BF16).reshape(N_EXP, 16, width)
    pl.semaphore_wait(barrier, N_EXP + 3)

    def across(source, target, k, sems):
        return pltpu.make_async_remote_copy(
            src_ref=source.at[(me_e + k) % N_EXP],
            dst_ref=target.at[me_e],
            send_sem=sems[0].at[k],
            recv_sem=sems[1].at[k],
            device_id={"expert": (me_e + k) % N_EXP},
            device_id_type=MESH,
        )

    def exchange(source, target, sems):
        own = pltpu.make_async_copy(source.at[me_e], target.at[me_e], sems[0].at[0])
        own.start()

        def go(k, carry):
            across(source, target, k, sems).start()
            return carry

        def done(k, carry):
            across(source, target, k, sems).wait()
            return carry

        lax.fori_loop(1, N_EXP, go, 0)
        own.wait()
        lax.fori_loop(1, N_EXP, done, 0)

    exchange(send, recv, (a2a_send, a2a_recv))

    row = lax.broadcasted_iota(jnp.int32, (128, 128), 0)
    source_row = ((row & 31) >> 2) * 16 + ((row >> 5) & 1) * 8 + (row >> 6) * 4 + (row & 3)
    shuffle = onehot(source_row == lane)
    block = dot(shuffle, recv[...].reshape(128, width), 1, 0).astype(BF16)
    for c in range(2):
        for a in range(2):
            gathered[c, a, HALF] = block[(c * 2 + a) * 32 : (c * 2 + a + 1) * 32]

    def gather_copy(c, d, a, s):
        return pltpu.make_async_remote_copy(
            src_ref=gathered.at[c, a, HALF + 1 - s if d == 0 else HALF - 1 + s],
            dst_ref=gathered.at[c, a, HALF - s if d == 0 else (HALF + s) % N_DP],
            send_sem=ag_send.at[c, d, a, s - 1],
            recv_sem=ag_recv.at[c, d, a, s - 1],
            device_id={"dp": near[c][d]},
            device_id_type=MESH,
        )

    def experts(c, rows, grads):
        count = rows.shape[0]
        pre = dot(rows, w_in[c], 1, 0)
        erf = 1.0 + lax.erf(pre * inv_root_two)
        hid = (0.5 * pre * erf).astype(BF16)
        slope = 0.5 * erf + pre * jnp.exp(-0.5 * pre * pre) * inv_root_two_pi
        grad = (dot(grads, w_out[c], 1, 1) * slope).astype(BF16)
        out = dot(hid, w_out[c], 1, 0).astype(BF16)
        row_grad = dot(grad, w_in[c], 1, 1).astype(BF16)
        shape = (count // 32, 32, -1)
        return [v.reshape(shape) for v in (hid, grad, out, row_grad)]

    def keep(c, at, values, first):
        hid, grad, out, row_grad = (v[first : first + at.size] for v in values)
        hidden[c, at] = hid
        pre_grad[c, at] = grad
        part[c, 0, at] = out
        part[c, 1, at] = row_grad

    def gather_step(s, carry):
        @pl.when(s <= HALF)
        def _():
            for a in range(2):
                for c in range(2):
                    for d in range(2):
                        @pl.when(s > 1)
                        def _():
                            gather_copy(c, d, a, s - 1).wait_recv()

                        if d == a:
                            gather_copy(c, d, a, s).start()
                        else:
                            @pl.when(s < HALF)
                            def _():
                                gather_copy(c, d, a, s).start()

        @pl.when(s == 2)
        def _():
            load_in.wait()
            load_out.wait()

        @pl.when(s > 1)
        def _():
            c = s % 2
            base = s - 2 - c
            behind, ahead = pl.ds(HALF - 1 - base, 2), pl.ds(HALF + base, 2)

            def both(a):
                return jnp.concatenate(
                    [gathered[c, a, behind].reshape(64, width), gathered[c, a, ahead].reshape(64, width)]
                )

            values = experts(c, both(0), both(1))
            keep(c, behind, values, 0)
            keep(c, ahead, values, 2)

        return carry

    lax.fori_loop(1, HALF + 2, gather_step, 0)
    for c in range(2):
        for a in range(2):
            gather_copy(c, a, a, HALF).wait_recv()
        keep(c, pl.ds(0, 1), experts(c, gathered[c, 0, 0], gathered[c, 1, 0]), 0)

    def sum_slot(d, t):
        return (N_DP + 1 - t) % N_DP if d == 0 else t - 1

    def sum_copy(c, d, a, t):
        return pltpu.make_async_remote_copy(
            src_ref=part.at[c, a, sum_slot(d, t)],
            dst_ref=arrived.at[c, a, N_DP - t if d == 0 else t % HALF],
            send_sem=rs_send.at[c, d, a, t - 1],
            recv_sem=rs_recv.at[c, d, a, t - 1],
            device_id={"dp": near[c][d]},
            device_id_type=MESH,
        )

    def sum_step(t, carry):
        for a in range(2):
            for c in range(2):
                for d in range(2):
                    first = 1 if d == a else 2

                    @pl.when(t > first)
                    def _():
                        sum_copy(c, d, a, t - 1).wait_recv()
                        slot = sum_slot(d, t)
                        part[c, a, slot] = (
                            part[c, a, slot].astype(F32) + arrived[c, a, slot].astype(F32)
                        ).astype(BF16)

                    @pl.when(t >= first)
                    def _():
                        sum_copy(c, d, a, t).start()

        @pl.when(t <= width // 128)
        def _():
            cut = pl.ds(pl.multiple_of((t - 1) * 128, 128), 128)
            for c in range(2):
                w_in_grad[c, cut, :] = dot(
                    gathered[c, 0, :, :, cut].reshape(1024, 128), pre_grad[c].reshape(1024, -1), 0, 0
                )
                w_out_grad[c, :, cut] = dot(
                    hidden[c].reshape(1024, -1), gathered[c, 1, :, :, cut].reshape(1024, 128), 0, 0
                )

        return carry

    lax.fori_loop(1, HALF + 1, sum_step, 0)
    total = []
    for c in range(2):
        for a in range(2):
            for d in range(2):
                sum_copy(c, d, a, HALF).wait_recv()
            total.append(
                (
                    part[c, a, HALF].astype(F32)
                    + arrived[c, a, HALF].astype(F32)
                    + arrived[c, a, 0].astype(F32)
                ).astype(BF16)
            )
    send[...] = dot(shuffle, jnp.concatenate(total), 0, 0).astype(BF16).reshape(N_EXP, 16, width)
    exchange(send, back, (ret_send, ret_recv))

    returned = back[...].reshape(128, width)
    picked = [dot(onehot(pick[k]), returned, 1, 0) for k in range(2)]
    mixed[...] = (gates[:, 0:1] * picked[0] + gates[:, 1:2] * picked[1]).astype(BF16)
    gate_grad[...] = jnp.concatenate(
        [jnp.sum(picked[k] * grad_wide, axis=1, keepdims=True) for k in range(2)], axis=1
    )
    tok_grad[...] = dot(onehot(pick_grad[0] | pick_grad[1]), returned, 1, 0).astype(BF16)

    def drain(s, carry):
        for c in range(2):
            for d in range(2):
                for a in range(2):
                    if d == a:
                        gather_copy(c, d, a, s).wait_send()
                        sum_copy(c, d, a, s).wait_send()
                    else:
                        @pl.when(s < HALF)
                        def _():
                            gather_copy(c, d, a, s).wait_send()
                            sum_copy(c, d, a, s + 1).wait_send()
        return carry

    lax.fori_loop(1, HALF + 1, drain, 0)


def per_device(tokens, expert_ids, slot_ids, dropped, gates, w_in, w_out, out_grad):
    count, width = tokens.shape
    hidden_units = w_in.shape[2]
    vmem = pl.BlockSpec(memory_space=pltpu.VMEM)
    anywhere = pl.BlockSpec(memory_space=pl.ANY)
    blocks = pltpu.VMEM((2, 2, N_DP, 32, width), BF16)
    units = pltpu.VMEM((2, N_DP, 32, hidden_units), BF16)
    small = pltpu.VMEM((N_EXP, 16, width), BF16)
    dma = pltpu.SemaphoreType.DMA
    return pl.pallas_call(
        kernel,
        out_shape=(
            jax.ShapeDtypeStruct((count, width), BF16),
            jax.ShapeDtypeStruct((count, width), BF16),
            jax.ShapeDtypeStruct((count, 2), F32),
            jax.ShapeDtypeStruct(w_in.shape, F32),
            jax.ShapeDtypeStruct(w_out.shape, F32),
        ),
        in_specs=[vmem] * 6 + [anywhere] * 2,
        out_specs=[vmem] * 5,
        scratch_shapes=[
            blocks, blocks, blocks, units, units,
            pltpu.VMEM(w_in.shape, BF16), pltpu.VMEM(w_out.shape, BF16),
            small, small, small,
            dma((2,)), dma((N_EXP,)), dma((N_EXP,)),
            dma((2, 2, 2, HALF)), dma((2, 2, 2, HALF)), dma((2, 2, 2, HALF)), dma((2, 2, 2, HALF)),
            dma((N_EXP,)), dma((N_EXP,)),
        ],
        compiler_params=pltpu.CompilerParams(
            collective_id=0, has_side_effects=True, vmem_limit_bytes=60 * 1024 * 1024
        ),
        cost_estimate=pl.CostEstimate(
            flops=12 * 2048 * width * hidden_units, bytes_accessed=20_000_000, transcendentals=2_000_000
        ),
    )(tokens, expert_ids, slot_ids, dropped, gates, out_grad, w_in, w_out)


def solution(mesh):
    rows = P(("expert", "dp"), None)
    placed = (rows, rows, rows, rows, rows, P("expert", None, "dp"), P("expert", "dp", None), rows)
    return jax.shard_map(
        per_device,
        mesh=mesh,
        in_specs=placed,
        out_specs=(rows, rows, rows, P("expert", None, "dp"), P("expert", "dp", None)),
        check_vma=False,
    )
```

```python
import jax
import jax.numpy as jnp
from jax import lax
from jax.experimental import pallas as pl
from jax.experimental.pallas import tpu as pltpu
from jax.sharding import PartitionSpec as P

CAP = 4
N_EXP = 8
N_DP = 32
HALF = 16
BF16 = jnp.bfloat16
F32 = jnp.float32
MESH = pl.DeviceIdType.MESH

inv_root_two = 0.7071067811865476
inv_root_two_pi = 0.3989422804014327


def place_first(y, z):
    return 4 * z + (y + z) % 4


def device_first(p):
    z = p // 4
    return ((p % 4 + 8 - z) % 4) * 8 + z


def place_second(y, z):
    w = (z + 24 - 3 * y) % 8
    return 4 * y + 16 * (w // 4) + w % 4


def device_second(p):
    q = p // 4
    return (q % 4) * 8 + (3 * q + p % 4) % 8


def dot(left, right, left_dim, right_dim):
    return lax.dot_general(
        left, right, (((left_dim,), (right_dim,)), ((), ())), preferred_element_type=F32
    )


def kernel(
    tokens, ids, slots, dropped, gates, out_grad, w_in_hbm, w_out_hbm,
    mixed, tok_grad, gate_grad, w_in_grad, w_out_grad,
    gathered, part, arrived, hidden, pre_grad, w_in, w_out, send, recv, back,
    load_sem, a2a_send, a2a_recv, ag_send, ag_recv, rs_send, rs_recv, ret_send, ret_recv,
):
    width = tokens.shape[1]
    left = send.shape[3]
    me_e = lax.axis_index("expert")
    me_d = lax.axis_index("dp")
    y, z = me_d // 8, me_d % 8
    here = (place_first(y, z), place_second(y, z))
    device = (device_first, device_second)
    near = [[device[c]((here[c] + step) % N_DP) for step in (1, N_DP - 1)] for c in range(2)]

    def beside(c, d):
        return {"dp": near[0][d] + c * (near[1][d] - near[0][d])}

    load_in = pltpu.make_async_copy(w_in_hbm, w_in, load_sem.at[0])
    load_out = pltpu.make_async_copy(w_out_hbm, w_out, load_sem.at[1])
    load_in.start()
    load_out.start()

    barrier = pltpu.get_barrier_semaphore()

    def greet(k, carry):
        pl.semaphore_signal(
            barrier, inc=1, device_id={"expert": (me_e + k) % N_EXP}, device_id_type=MESH
        )
        return carry

    lax.fori_loop(1, N_EXP, greet, 0)
    for c in range(2):
        for d in range(2):
            pl.semaphore_signal(barrier, inc=1, device_id={"dp": near[c][d]}, device_id_type=MESH)

    expert = ids[...]
    column = (expert >> 1) * 16 + (expert & 1) * 4 + slots[...]
    column = jnp.where(dropped[...] == 0, column, -64)
    row = lax.broadcasted_iota(jnp.int32, (128, 128), 0)
    lane = lax.broadcasted_iota(jnp.int32, (128, 128), 1)

    def onehot(mask):
        return jnp.where(mask, 1.0, 0.0).astype(BF16)

    chosen = [[onehot(column[k : k + 1, :] + 8 * h == row) for h in range(2)] for k in range(2)]
    gate = [jnp.broadcast_to(gates[k : k + 1, :], (128, 128)).T[:, :1] for k in range(2)]
    pad = 2 * left - width

    def halves(value):
        zeros = jnp.zeros((value.shape[0], pad), BF16)
        return value[:, :left], jnp.concatenate([value[:, left:], zeros], axis=1)

    def pack(a, values):
        packed = sum(dot(chosen[k][h], values[k][h], 1, 0) for k in range(2) for h in range(2))
        send[a] = packed.astype(BF16).reshape(N_EXP, 16, left)

    def across(source, target, a, k, sems):
        return pltpu.make_async_remote_copy(
            src_ref=source.at[a, (me_e + k) % N_EXP],
            dst_ref=target.at[a, me_e],
            send_sem=sems[0].at[a, k],
            recv_sem=sems[1].at[a, k],
            device_id={"expert": (me_e + k) % N_EXP},
            device_id_type=MESH,
        )

    def exchange_start(source, target, a, sems):
        def go(k, carry):
            across(source, target, a, k, sems).start()
            return carry

        lax.fori_loop(1, N_EXP, go, 0)
        target[a, me_e] = source[a, me_e]

    def exchange_wait(source, target, a, sems):
        def done(k, carry):
            across(source, target, a, k, sems).wait()
            return carry

        lax.fori_loop(1, N_EXP, done, 0)

    out_way = (a2a_send, a2a_recv)
    token_halves = halves(tokens[...])
    pack(0, (token_halves, token_halves))
    pl.semaphore_wait(barrier, N_EXP + 3)
    exchange_start(send, recv, 0, out_way)
    pack(1, [halves((gate[k] * out_grad[...].astype(F32)).astype(BF16)) for k in range(2)])
    exchange_start(send, recv, 1, out_way)

    out_row = row[:64]
    source_row = ((out_row & 31) >> 2) * 16 + (out_row >> 5) * 4 + (out_row & 3)
    shuffle = [onehot(source_row + 8 * h == lane[:64]) for h in range(2)]

    def gather_copy(c, d, a, s):
        return pltpu.make_async_remote_copy(
            src_ref=gathered.at[c, a, HALF + 1 - s if d == 0 else HALF - 1 + s],
            dst_ref=gathered.at[c, a, HALF - s if d == 0 else (HALF + s) % N_DP],
            send_sem=ag_send.at[c, d, a, s - 1],
            recv_sem=ag_recv.at[c, d, a, s - 1],
            device_id=beside(c, d),
            device_id_type=MESH,
        )

    for a in range(2):
        exchange_wait(send, recv, a, out_way)
        got = recv[a].reshape(128, left)
        for h in range(2):
            block = dot(shuffle[h], got, 1, 0).astype(BF16)
            for c in range(2):
                if h == 0:
                    gathered[c, a, HALF, :, :left] = block[c * 32 : (c + 1) * 32]
                else:
                    gathered[c, a, HALF, :, left:] = block[c * 32 : (c + 1) * 32, : width - left]
        for c in range(2):
            for d in range(2):
                gather_copy(c, d, a, 1).start()

    def experts(c, rows, grads):
        count = rows.shape[0]
        pre = dot(rows, w_in[c], 1, 0)
        erf = 1.0 + lax.erf(pre * inv_root_two)
        hid = (0.5 * pre * erf).astype(BF16)
        slope = 0.5 * erf + pre * jnp.exp(-0.5 * pre * pre) * inv_root_two_pi
        grad = (dot(grads, w_out[c], 1, 1) * slope).astype(BF16)
        out = dot(hid, w_out[c], 1, 0).astype(BF16)
        row_grad = dot(grad, w_in[c], 1, 1).astype(BF16)
        shape = (count // 32, 32, -1)
        return [v.reshape(shape) for v in (hid, grad, out, row_grad)]

    def keep(c, at, values, first):
        hid, grad, out, row_grad = (v[first : first + at.size] for v in values)
        hidden[c, at] = hid
        pre_grad[c, at] = grad
        part[c, 0, at] = out
        part[c, 1, at] = row_grad

    def sum_slot(d, t):
        return (N_DP + 1 - t) % N_DP if d == 0 else t - 1

    def sum_copy(c, d, a, t):
        return pltpu.make_async_remote_copy(
            src_ref=part.at[c, a, sum_slot(d, t)],
            dst_ref=arrived.at[c, a, N_DP - t if d == 0 else t % HALF],
            send_sem=rs_send.at[c, d, a, t - 1],
            recv_sem=rs_recv.at[c, d, a, t - 1],
            device_id=beside(c, d),
            device_id_type=MESH,
        )

    def gather_step(s, carry):
        @pl.when(s <= HALF)
        def _():
            for a in range(2):
                for c in range(2):
                    for d in range(2):
                        gather_copy(c, d, a, s - 1).wait_recv()
                        if d == a:
                            gather_copy(c, d, a, s).start()
                        else:
                            @pl.when(s < HALF)
                            def _():
                                gather_copy(c, d, a, s).start()

        @pl.when(s == 2)
        def _():
            load_in.wait()
            load_out.wait()

        c = s % 2
        base = s - 2 - c
        behind, ahead = pl.ds(HALF - 1 - base, 2), pl.ds(HALF + base, 2)

        def both(a):
            return jnp.concatenate(
                [gathered[c, a, behind].reshape(64, width), gathered[c, a, ahead].reshape(64, width)]
            )

        values = experts(c, both(0), both(1))
        keep(c, behind, values, 0)
        keep(c, ahead, values, 2)

        @pl.when(s >= HALF)
        def _():
            for a in range(2):
                sum_copy(c, 1 - a, a, 2).start()

        return carry

    lax.fori_loop(2, HALF + 2, gather_step, 0)
    for c in range(2):
        for a in range(2):
            gather_copy(c, a, a, HALF).wait_recv()
        keep(c, pl.ds(0, 1), experts(c, gathered[c, 0, 0], gathered[c, 1, 0]), 0)
        for a in range(2):
            sum_copy(c, a, a, 1).start()

    def add(c, d, a, t):
        sum_copy(c, d, a, t - 1).wait_recv()
        slot = sum_slot(d, t)
        part[c, a, slot] = (part[c, a, slot].astype(F32) + arrived[c, a, slot].astype(F32)).astype(BF16)
        sum_copy(c, d, a, t).start()

    def sum_step(t, carry):
        for c in range(2):
            for a in range(2):
                @pl.when(t < HALF)
                def _():
                    add(c, 1 - a, a, t + 1)

        for c in range(2):
            for a in range(2):
                add(c, a, a, t)

        @pl.when(t <= width // 128 + 1)
        def _():
            cut = pl.ds(pl.multiple_of((t - 2) * 128, 128), 128)
            for c in range(2):
                w_in_grad[c, cut, :] = dot(
                    gathered[c, 0, :, :, cut].reshape(1024, 128), pre_grad[c].reshape(1024, -1), 0, 0
                )
                w_out_grad[c, :, cut] = dot(
                    hidden[c].reshape(1024, -1), gathered[c, 1, :, :, cut].reshape(1024, 128), 0, 0
                )

        return carry

    lax.fori_loop(2, HALF + 1, sum_step, 0)
    home = (ret_send, ret_recv)
    for a in range(2):
        total = []
        for c in range(2):
            for d in range(2):
                sum_copy(c, d, a, HALF).wait_recv()
            total.append(
                (
                    part[c, a, HALF].astype(F32)
                    + arrived[c, a, HALF].astype(F32)
                    + arrived[c, a, 0].astype(F32)
                ).astype(BF16)
            )
        total = halves(jnp.concatenate(total))
        packed = sum(dot(shuffle[h], total[h], 0, 0) for h in range(2))
        send[a] = packed.astype(BF16).reshape(N_EXP, 16, left)
        exchange_start(send, back, a, home)

    def drain(s, carry):
        for c in range(2):
            for d in range(2):
                for a in range(2):
                    if d == a:
                        gather_copy(c, d, a, s).wait_send()
                        sum_copy(c, d, a, s).wait_send()
                    else:
                        @pl.when(s < HALF)
                        def _():
                            gather_copy(c, d, a, s).wait_send()
                            sum_copy(c, d, a, s + 1).wait_send()
        return carry

    lax.fori_loop(1, HALF + 1, drain, 0)

    def unpack(a, k):
        returned = back[a].reshape(128, left)
        first, second = (dot(chosen[k][h], returned, 0, 0) for h in range(2))
        return jnp.concatenate([first, second[:, : width - left]], axis=1)

    exchange_wait(send, back, 0, home)
    grad_wide = out_grad[...].astype(F32)
    picked = [unpack(0, k) for k in range(2)]
    mixed[...] = (gate[0] * picked[0] + gate[1] * picked[1]).astype(BF16)
    for k in range(2):
        inner = jnp.sum(picked[k] * grad_wide, axis=1, keepdims=True)
        gate_grad[k : k + 1, :] = jnp.broadcast_to(inner, (128, 128)).T[:1]
    exchange_wait(send, back, 1, home)
    tok_grad[...] = (unpack(1, 0) + unpack(1, 1)).astype(BF16)


def per_device(tokens, expert_ids, slot_ids, dropped, gates, w_in, w_out, out_grad):
    count, width = tokens.shape
    hidden_units = w_in.shape[2]
    vmem = pl.BlockSpec(memory_space=pltpu.VMEM)
    anywhere = pl.BlockSpec(memory_space=pl.ANY)
    blocks = pltpu.VMEM((2, 2, N_DP, 32, width), BF16)
    units = pltpu.VMEM((2, N_DP, 32, hidden_units), BF16)
    small = pltpu.VMEM((2, N_EXP, 16, (width // 128 + 1) // 2 * 128), BF16)
    dma = pltpu.SemaphoreType.DMA
    mixed, tok_grad, gate_grad, w_in_grad, w_out_grad = pl.pallas_call(
        kernel,
        out_shape=(
            pltpu.VMEM((count, width), BF16),
            pltpu.VMEM((count, width), BF16),
            pltpu.VMEM((2, count), F32),
            pltpu.VMEM(w_in.shape, F32),
            pltpu.VMEM(w_out.shape, F32),
        ),
        in_specs=[vmem] * 6 + [anywhere] * 2,
        scratch_shapes=[
            blocks, blocks, blocks, units, units,
            pltpu.VMEM(w_in.shape, BF16), pltpu.VMEM(w_out.shape, BF16),
            small, small, small,
            dma((2,)), dma((2, N_EXP)), dma((2, N_EXP)),
            dma((2, 2, 2, HALF)), dma((2, 2, 2, HALF)), dma((2, 2, 2, HALF)), dma((2, 2, 2, HALF)),
            dma((2, N_EXP)), dma((2, N_EXP)),
        ],
        compiler_params=pltpu.CompilerParams(
            collective_id=0, has_side_effects=True, vmem_limit_bytes=50 * 1024 * 1024
        ),
        cost_estimate=pl.CostEstimate(
            flops=12 * 2048 * width * hidden_units, bytes_accessed=20_000_000, transcendentals=2_000_000
        ),
    )(tokens, expert_ids.T, slot_ids.T, dropped.T, gates.T, out_grad, w_in, w_out)
    return mixed, tok_grad, gate_grad.T, w_in_grad, w_out_grad


def solution(mesh):
    rows = P(("expert", "dp"), None)
    placed = (rows, rows, rows, rows, rows, P("expert", None, "dp"), P("expert", "dp", None), rows)
    return jax.shard_map(
        per_device,
        mesh=mesh,
        in_specs=placed,
        out_specs=(rows, rows, rows, P("expert", None, "dp"), P("expert", "dp", None)),
        check_vma=False,
    )
```

```python
import jax
import jax.numpy as jnp
from jax import lax
from jax.experimental import pallas as pl
from jax.experimental.pallas import tpu as pltpu
from jax.sharding import PartitionSpec as P

CAP = 4
N_EXP = 8
N_DP = 32
HALF = 16
BF16 = jnp.bfloat16
F32 = jnp.float32
MESH = pl.DeviceIdType.MESH
ORDER = [(a, h, c, d) for a in range(2) for h in range(2) for c in range(2) for d in range(2)]

inv_root_two = 0.7071067811865476
inv_root_two_pi = 0.3989422804014327


def place_first(y, z):
    return 4 * z + (y + z) % 4


def device_first(p):
    z = p // 4
    return ((p % 4 + 8 - z) % 4) * 8 + z


def place_second(y, z):
    w = (z + 24 - 3 * y) % 8
    return 4 * y + 16 * (w // 4) + w % 4


def device_second(p):
    q = p // 4
    return (q % 4) * 8 + (3 * q + p % 4) % 8


def dot(left, right, left_dim, right_dim):
    return lax.dot_general(
        left, right, (((left_dim,), (right_dim,)), ((), ())), preferred_element_type=F32
    )


def kernel(
    tokens_in, ids_in, slots_in, dropped_in, gates_in, out_grad_in, w_in_in, w_out_in,
    mixed, tok_grad, gate_grad, w_in_grad, w_out_grad,
    tokens, ids, slots, dropped, gates, out_grad, w_in, w_out,
    gathered, part, arrived, hidden, pre_grad, send, recv, back,
    load_sem, a2a_send, a2a_recv, ag_send, ag_recv, rs_send, rs_recv, ret_send, ret_recv,
):
    width = tokens.shape[1]
    left = send.shape[3]
    me_e = lax.axis_index("expert")
    me_d = lax.axis_index("dp")
    y, z = me_d // 8, me_d % 8
    here = (place_first(y, z), place_second(y, z))
    device = (device_first, device_second)
    near = [[device[c]((here[c] + step) % N_DP) for step in (1, N_DP - 1)] for c in range(2)]

    def beside(c, d):
        return {"dp": near[0][d] + c * (near[1][d] - near[0][d])}

    barrier = pltpu.get_barrier_semaphore()

    def greet(k, carry):
        pl.semaphore_signal(
            barrier, inc=1, device_id={"expert": (me_e + k) % N_EXP}, device_id_type=MESH
        )
        return carry

    lax.fori_loop(1, N_EXP, greet, 0)
    for c in range(2):
        for d in range(2):
            pl.semaphore_signal(barrier, inc=1, device_id={"dp": near[c][d]}, device_id_type=MESH)

    loads = [
        pltpu.make_async_copy(source, target, load_sem.at[i])
        for i, (source, target) in enumerate(
            (
                (ids_in, ids), (slots_in, slots), (dropped_in, dropped), (tokens_in, tokens),
                (gates_in, gates), (out_grad_in, out_grad), (w_in_in, w_in), (w_out_in, w_out),
            )
        )
    ]
    for load in loads:
        load.start()
    for load in loads[:4]:
        load.wait()

    expert = ids[...]
    column = (expert >> 1) * 16 + (expert & 1) * 4 + slots[...]
    column = jnp.where(dropped[...] == 0, column, -64)
    row = lax.broadcasted_iota(jnp.int32, (128, 128), 0)
    lane = lax.broadcasted_iota(jnp.int32, (128, 128), 1)

    def onehot(mask):
        return jnp.where(mask, 1.0, 0.0).astype(BF16)

    chosen = [[onehot(column[k : k + 1, :] + 8 * h == row) for h in range(2)] for k in range(2)]
    pad = 2 * left - width

    def halves(value):
        zeros = jnp.zeros((value.shape[0], pad), BF16)
        return value[:, :left], jnp.concatenate([value[:, left:], zeros], axis=1)

    def pack(a, values):
        packed = sum(dot(chosen[k][h], values[k][h], 1, 0) for k in range(2) for h in range(2))
        send[a] = packed.astype(BF16).reshape(N_EXP, 16, left)

    def across(source, target, a, k, sems):
        return pltpu.make_async_remote_copy(
            src_ref=source.at[a, (me_e + k) % N_EXP],
            dst_ref=target.at[a, me_e],
            send_sem=sems[0].at[a, k],
            recv_sem=sems[1].at[a, k],
            device_id={"expert": (me_e + k) % N_EXP},
            device_id_type=MESH,
        )

    def exchange_start(source, target, a, sems):
        def go(k, carry):
            across(source, target, a, k, sems).start()
            return carry

        lax.fori_loop(1, N_EXP, go, 0)
        target[a, me_e] = source[a, me_e]

    def exchange_wait(source, target, a, sems):
        def done(k, carry):
            across(source, target, a, k, sems).wait()
            return carry

        lax.fori_loop(1, N_EXP, done, 0)

    out_way = (a2a_send, a2a_recv)
    token_halves = halves(tokens[...])
    pack(0, (token_halves, token_halves))
    pl.semaphore_wait(barrier, N_EXP + 3)
    exchange_start(send, recv, 0, out_way)
    for load in loads[4:6]:
        load.wait()
    gate = [jnp.broadcast_to(gates[k : k + 1, :], (128, 128)).T[:, :1] for k in range(2)]
    pack(1, [halves((gate[k] * out_grad[...].astype(F32)).astype(BF16)) for k in range(2)])
    exchange_start(send, recv, 1, out_way)

    out_row = row[:64]
    source_row = ((out_row & 31) >> 2) * 16 + (out_row >> 5) * 4 + (out_row & 3)
    shuffle = [onehot(source_row + 8 * h == lane[:64]) for h in range(2)]

    def gather_copy(c, d, a, h, s):
        rows = pl.ds(h * 16, 16)
        return pltpu.make_async_remote_copy(
            src_ref=gathered.at[c, a, HALF + 1 - s if d == 0 else HALF - 1 + s, rows],
            dst_ref=gathered.at[c, a, HALF - s if d == 0 else (HALF + s) % N_DP, rows],
            send_sem=ag_send.at[c, d, 2 * a + h, s - 1],
            recv_sem=ag_recv.at[c, d, 2 * a + h, s - 1],
            device_id=beside(c, d),
            device_id_type=MESH,
        )

    for a in range(2):
        exchange_wait(send, recv, a, out_way)
        got = recv[a].reshape(128, left)
        for h in range(2):
            block = dot(shuffle[h], got, 1, 0).astype(BF16)
            for c in range(2):
                if h == 0:
                    gathered[c, a, HALF, :, :left] = block[c * 32 : (c + 1) * 32]
                else:
                    gathered[c, a, HALF, :, left:] = block[c * 32 : (c + 1) * 32, : width - left]
        for h in range(2):
            for c in range(2):
                for d in range(2):
                    gather_copy(c, d, a, h, 1).start()

    def experts(c, rows, grads):
        count = rows.shape[0]
        pre = dot(rows, w_in[c], 1, 0)
        erf = 1.0 + lax.erf(pre * inv_root_two)
        hid = (0.5 * pre * erf).astype(BF16)
        slope = 0.5 * erf + pre * jnp.exp(-0.5 * pre * pre) * inv_root_two_pi
        grad = (dot(grads, w_out[c], 1, 1) * slope).astype(BF16)
        out = dot(hid, w_out[c], 1, 0).astype(BF16)
        row_grad = dot(grad, w_in[c], 1, 1).astype(BF16)
        shape = (count // 32, 32, -1)
        return [v.reshape(shape) for v in (hid, grad, out, row_grad)]

    def keep(c, at, values, first):
        hid, grad, out, row_grad = (v[first : first + at.size] for v in values)
        hidden[c, at] = hid
        pre_grad[c, at] = grad
        part[c, 0, at] = out
        part[c, 1, at] = row_grad

    def sum_slot(d, t):
        return (N_DP + 1 - t) % N_DP if d == 0 else t - 1

    def sum_copy(c, d, a, h, t):
        rows = pl.ds(h * 16, 16)
        return pltpu.make_async_remote_copy(
            src_ref=part.at[c, a, sum_slot(d, t), rows],
            dst_ref=arrived.at[c, a, N_DP - t if d == 0 else t % HALF, rows],
            send_sem=rs_send.at[c, d, 2 * a + h, t - 1],
            recv_sem=rs_recv.at[c, d, 2 * a + h, t - 1],
            device_id=beside(c, d),
            device_id_type=MESH,
        )

    def gather_step(s, carry):
        @pl.when(s <= HALF)
        def _():
            for a, h, c, d in ORDER:
                gather_copy(c, d, a, h, s - 1).wait_recv()
                if d == a:
                    gather_copy(c, d, a, h, s).start()
                else:
                    @pl.when(s < HALF)
                    def _():
                        gather_copy(c, d, a, h, s).start()

        @pl.when(s == 2)
        def _():
            for load in loads[6:]:
                load.wait()

        c = s % 2
        base = s - 2 - c
        behind, ahead = pl.ds(HALF - 1 - base, 2), pl.ds(HALF + base, 2)

        def both(a):
            return jnp.concatenate(
                [gathered[c, a, behind].reshape(64, width), gathered[c, a, ahead].reshape(64, width)]
            )

        values = experts(c, both(0), both(1))
        keep(c, behind, values, 0)
        keep(c, ahead, values, 2)

        @pl.when(s >= HALF)
        def _():
            for a in range(2):
                for h in range(2):
                    sum_copy(c, 1 - a, a, h, 2).start()

        return carry

    lax.fori_loop(2, HALF + 2, gather_step, 0)
    for c in range(2):
        for a in range(2):
            for h in range(2):
                gather_copy(c, a, a, h, HALF).wait_recv()
        keep(c, pl.ds(0, 1), experts(c, gathered[c, 0, 0], gathered[c, 1, 0]), 0)
        for a in range(2):
            for h in range(2):
                sum_copy(c, a, a, h, 1).start()

    def add(c, d, a, h, t):
        sum_copy(c, d, a, h, t - 1).wait_recv()
        at = (c, a, sum_slot(d, t), pl.ds(h * 16, 16))
        part[at] = (part[at].astype(F32) + arrived[at].astype(F32)).astype(BF16)
        sum_copy(c, d, a, h, t).start()

    def sum_step(t, carry):
        for a, h, c, d in ORDER:
            if d != a:
                @pl.when(t < HALF)
                def _():
                    add(c, d, a, h, t + 1)

        for a, h, c, d in ORDER:
            if d == a:
                add(c, d, a, h, t)

        @pl.when(t <= width // 128 + 1)
        def _():
            cut = pl.ds(pl.multiple_of((t - 2) * 128, 128), 128)
            for c in range(2):
                w_in_grad[c, cut, :] = dot(
                    gathered[c, 0, :, :, cut].reshape(1024, 128), pre_grad[c].reshape(1024, -1), 0, 0
                )
                w_out_grad[c, :, cut] = dot(
                    hidden[c].reshape(1024, -1), gathered[c, 1, :, :, cut].reshape(1024, 128), 0, 0
                )

        return carry

    lax.fori_loop(2, HALF + 1, sum_step, 0)
    home = (ret_send, ret_recv)
    for a in range(2):
        total = []
        for c in range(2):
            for d in range(2):
                for h in range(2):
                    sum_copy(c, d, a, h, HALF).wait_recv()
            total.append(
                (
                    part[c, a, HALF].astype(F32)
                    + arrived[c, a, HALF].astype(F32)
                    + arrived[c, a, 0].astype(F32)
                ).astype(BF16)
            )
        total = halves(jnp.concatenate(total))
        packed = sum(dot(shuffle[h], total[h], 0, 0) for h in range(2))
        send[a] = packed.astype(BF16).reshape(N_EXP, 16, left)
        exchange_start(send, back, a, home)

    def drain(s, carry):
        for a, h, c, d in ORDER:
            if d == a:
                gather_copy(c, d, a, h, s).wait_send()
                sum_copy(c, d, a, h, s).wait_send()
            else:
                @pl.when(s < HALF)
                def _():
                    gather_copy(c, d, a, h, s).wait_send()
                    sum_copy(c, d, a, h, s + 1).wait_send()
        return carry

    lax.fori_loop(1, HALF + 1, drain, 0)

    def unpack(a, k):
        returned = back[a].reshape(128, left)
        first, second = (dot(chosen[k][h], returned, 0, 0) for h in range(2))
        return jnp.concatenate([first, second[:, : width - left]], axis=1)

    exchange_wait(send, back, 0, home)
    grad_wide = out_grad[...].astype(F32)
    picked = [unpack(0, k) for k in range(2)]
    mixed[...] = (gate[0] * picked[0] + gate[1] * picked[1]).astype(BF16)
    for k in range(2):
        inner = jnp.sum(picked[k] * grad_wide, axis=1, keepdims=True)
        gate_grad[k : k + 1, :] = jnp.broadcast_to(inner, (128, 128)).T[:1]
    exchange_wait(send, back, 1, home)
    tok_grad[...] = (unpack(1, 0) + unpack(1, 1)).astype(BF16)


def write_back(*refs):
    sems = refs[-1]
    copies = []
    for i in (3, 4, 0, 1, 2):
        source, target = refs[i], refs[5 + i]
        if len(source.shape) == 3:
            copies += [pltpu.make_async_copy(source.at[c], target.at[c], sems.at[i, c]) for c in range(2)]
        else:
            copies.append(pltpu.make_async_copy(source, target, sems.at[i, 0]))
    for copy in copies:
        copy.start()
    for copy in copies:
        copy.wait()


def per_device(tokens, expert_ids, slot_ids, dropped, gates, w_in, w_out, out_grad):
    count, width = tokens.shape
    hidden_units = w_in.shape[2]
    anywhere = pl.BlockSpec(memory_space=pl.ANY)
    blocks = pltpu.VMEM((2, 2, N_DP, 32, width), BF16)
    units = pltpu.VMEM((2, N_DP, 32, hidden_units), BF16)
    small = pltpu.VMEM((2, N_EXP, 16, (width // 128 + 1) // 2 * 128), BF16)
    dma = pltpu.SemaphoreType.DMA
    results = pl.pallas_call(
        kernel,
        out_shape=(
            pltpu.VMEM((count, width), BF16),
            pltpu.VMEM((count, width), BF16),
            pltpu.VMEM((2, count), F32),
            pltpu.VMEM(w_in.shape, F32),
            pltpu.VMEM(w_out.shape, F32),
        ),
        in_specs=[anywhere] * 8,
        scratch_shapes=[
            pltpu.VMEM((count, width), BF16),
            *[pltpu.VMEM((2, count), jnp.int32)] * 3,
            pltpu.VMEM((2, count), F32),
            pltpu.VMEM((count, width), BF16),
            pltpu.VMEM(w_in.shape, BF16), pltpu.VMEM(w_out.shape, BF16),
            blocks, blocks, blocks, units, units, small, small, small,
            dma((8,)), dma((2, N_EXP)), dma((2, N_EXP)),
            *[dma((2, 2, 4, HALF))] * 4,
            dma((2, N_EXP)), dma((2, N_EXP)),
        ],
        compiler_params=pltpu.CompilerParams(
            collective_id=0, has_side_effects=True, vmem_limit_bytes=50 * 1024 * 1024
        ),
        cost_estimate=pl.CostEstimate(
            flops=12 * 2048 * width * hidden_units, bytes_accessed=20_000_000, transcendentals=2_000_000
        ),
    )(tokens, expert_ids.T, slot_ids.T, dropped.T, gates.T, out_grad, w_in, w_out)
    mixed, tok_grad, gate_grad, w_in_grad, w_out_grad = pl.pallas_call(
        write_back,
        out_shape=[jax.ShapeDtypeStruct(v.shape, v.dtype) for v in results],
        in_specs=[anywhere] * 5,
        out_specs=[anywhere] * 5,
        scratch_shapes=[dma((5, 2))],
        compiler_params=pltpu.CompilerParams(vmem_limit_bytes=1024 * 1024),
    )(*results)
    return mixed, tok_grad, gate_grad.T, w_in_grad, w_out_grad


def solution(mesh):
    rows = P(("expert", "dp"), None)
    placed = (rows, rows, rows, rows, rows, P("expert", None, "dp"), P("expert", "dp", None), rows)
    return jax.shard_map(
        per_device,
        mesh=mesh,
        in_specs=placed,
        out_specs=(rows, rows, rows, P("expert", None, "dp"), P("expert", "dp", None)),
        check_vma=False,
    )
```

```python
import jax
import jax.numpy as jnp
from jax import lax
from jax.experimental import pallas as pl
from jax.experimental.pallas import tpu as pltpu
from jax.sharding import PartitionSpec as P

CAP = 4
N_EXP = 8
N_DP = 32
HALF = 16
BF16 = jnp.bfloat16
F32 = jnp.float32
MESH = pl.DeviceIdType.MESH
ORDER = [(a, h, c, d) for a in range(2) for h in range(2) for c in range(2) for d in range(2)]

inv_root_two = 0.7071067811865476
inv_root_two_pi = 0.3989422804014327


def place_first(y, z):
    return 4 * z + (y + z) % 4


def device_first(p):
    z = p // 4
    return ((p % 4 + 8 - z) % 4) * 8 + z


def place_second(y, z):
    w = (z + 24 - 3 * y) % 8
    return 4 * y + 16 * (w // 4) + w % 4


def device_second(p):
    q = p // 4
    return (q % 4) * 8 + (3 * q + p % 4) % 8


def dot(left, right, left_dim, right_dim):
    return lax.dot_general(
        left, right, (((left_dim,), (right_dim,)), ((), ())), preferred_element_type=F32
    )


def kernel(
    tokens_in, ids_in, slots_in, dropped_in, gates_in, out_grad_in, w_in_in, w_out_in,
    mixed, tok_grad, gate_grad, w_in_grad, w_out_grad,
    tokens, ids, slots, dropped, gates, out_grad, w_in, w_out,
    gathered, part, arrived, hidden, pre_grad, send, recv, back,
    load_sem, a2a_send, a2a_recv, ag_send, ag_recv, rs_send, rs_recv, ret_send, ret_recv,
):
    width = tokens.shape[1]
    left = send.shape[3]
    me_e = lax.axis_index("expert")
    me_d = lax.axis_index("dp")
    y, z = me_d // 8, me_d % 8
    here = (place_first(y, z), place_second(y, z))
    device = (device_first, device_second)
    near = [[device[c]((here[c] + step) % N_DP) for step in (1, N_DP - 1)] for c in range(2)]

    def beside(c, d):
        return {"dp": near[0][d] + c * (near[1][d] - near[0][d])}

    barrier = pltpu.get_barrier_semaphore()

    def greet(k, carry):
        pl.semaphore_signal(
            barrier, inc=1, device_id={"expert": (me_e + k) % N_EXP}, device_id_type=MESH
        )
        return carry

    lax.fori_loop(1, N_EXP, greet, 0)
    for c in range(2):
        for d in range(2):
            pl.semaphore_signal(barrier, inc=1, device_id={"dp": near[c][d]}, device_id_type=MESH)

    loads = [
        pltpu.make_async_copy(source, target, load_sem.at[i])
        for i, (source, target) in enumerate(
            (
                (ids_in, ids), (slots_in, slots), (dropped_in, dropped), (tokens_in, tokens),
                (gates_in, gates), (out_grad_in, out_grad), (w_in_in, w_in), (w_out_in, w_out),
            )
        )
    ]
    for load in loads:
        load.start()
    for load in loads[:4]:
        load.wait()

    expert = ids[...]
    column = (expert >> 1) * 16 + (expert & 1) * 4 + slots[...]
    column = jnp.where(dropped[...] == 0, column, -64)
    row = lax.broadcasted_iota(jnp.int32, (128, 128), 0)
    lane = lax.broadcasted_iota(jnp.int32, (128, 128), 1)

    def onehot(mask):
        return jnp.where(mask, 1.0, 0.0).astype(BF16)

    def cut(value):
        zeros = jnp.zeros((value.shape[0], 2 * left - width), BF16)
        return [value[:, :left], jnp.concatenate([value[:, left:], zeros], axis=1)]

    chosen = [[column[k : k + 1, :] + 8 * h == row for h in range(2)] for k in range(2)]
    either = [chosen[0][h] | chosen[1][h] for h in range(2)]

    def pack(a, masks, values):
        masks = jnp.concatenate([onehot(mask) for mask in masks], axis=1)
        send[a] = dot(masks, jnp.concatenate(values), 1, 0).astype(BF16).reshape(N_EXP, 16, left)

    def across(source, target, a, k, sems):
        return pltpu.make_async_remote_copy(
            src_ref=source.at[a, (me_e + k) % N_EXP],
            dst_ref=target.at[a, me_e],
            send_sem=sems[0].at[a, k],
            recv_sem=sems[1].at[a, k],
            device_id={"expert": (me_e + k) % N_EXP},
            device_id_type=MESH,
        )

    far_first = (4, 3, 5, 2, 6, 1, 7)

    def exchange_start(source, target, a, sems):
        for k in far_first:
            across(source, target, a, k, sems).start()
        target[a, me_e] = source[a, me_e]

    def exchange_wait(source, target, a, sems):
        for k in reversed(far_first):
            across(source, target, a, k, sems).wait()

    out_way = (a2a_send, a2a_recv)
    pack(0, either, cut(tokens[...]))
    pl.semaphore_wait(barrier, N_EXP + 3)
    exchange_start(send, recv, 0, out_way)
    for load in loads[4:6]:
        load.wait()
    gate = [jnp.broadcast_to(gates[k : k + 1, :], (128, 128)).T[:, :1] for k in range(2)]
    scaled = [cut((gate[k] * out_grad[...].astype(F32)).astype(BF16)) for k in range(2)]
    pack(1, chosen[0] + chosen[1], scaled[0] + scaled[1])
    exchange_start(send, recv, 1, out_way)

    out_row = row[:64]
    source_row = ((out_row & 31) >> 2) * 16 + (out_row >> 5) * 4 + (out_row & 3)
    shuffle = [onehot(source_row + 8 * h == lane[:64]) for h in range(2)]

    def gather_copy(c, d, a, h, s):
        rows = pl.ds(h * 16, 16)
        return pltpu.make_async_remote_copy(
            src_ref=gathered.at[c, a, HALF + 1 - s if d == 0 else HALF - 1 + s, rows],
            dst_ref=gathered.at[c, a, HALF - s if d == 0 else (HALF + s) % N_DP, rows],
            send_sem=ag_send.at[c, d, 2 * a + h, s - 1],
            recv_sem=ag_recv.at[c, d, 2 * a + h, s - 1],
            device_id=beside(c, d),
            device_id_type=MESH,
        )

    for a in range(2):
        exchange_wait(send, recv, a, out_way)
        got = recv[a].reshape(128, left)
        for h in range(2):
            block = dot(shuffle[h], got, 1, 0).astype(BF16)
            for c in range(2):
                if h == 0:
                    gathered[c, a, HALF, :, :left] = block[c * 32 : (c + 1) * 32]
                else:
                    gathered[c, a, HALF, :, left:] = block[c * 32 : (c + 1) * 32, : width - left]
        for h in range(2):
            for c in range(2):
                for d in range(2):
                    gather_copy(c, d, a, h, 1).start()

    def turned(mask):
        return jnp.where(mask, 1.0, 0.0).T.astype(BF16)

    take = [[turned(chosen[k][h]) for h in range(2)] for k in range(2)]
    take_either = [turned(either[h]) for h in range(2)]
    block_row = lane & 63
    back_row = ((block_row & 31) >> 2) * 16 + (block_row >> 5) * 4 + (block_row & 3) + (lane >> 6) * 8
    unshuffle = onehot(back_row == row)

    def experts(c, rows, grads):
        count = rows.shape[0]
        pre = dot(rows, w_in[c], 1, 0)
        erf = 1.0 + lax.erf(pre * inv_root_two)
        hid = (0.5 * pre * erf).astype(BF16)
        slope = 0.5 * erf + pre * jnp.exp(-0.5 * pre * pre) * inv_root_two_pi
        grad = (dot(grads, w_out[c], 1, 1) * slope).astype(BF16)
        out = dot(hid, w_out[c], 1, 0).astype(BF16)
        row_grad = dot(grad, w_in[c], 1, 1).astype(BF16)
        shape = (count // 32, 32, -1)
        return [v.reshape(shape) for v in (hid, grad, out, row_grad)]

    def keep(c, at, values, first):
        hid, grad, out, row_grad = (v[first : first + at.size] for v in values)
        hidden[c, at] = hid
        pre_grad[c, at] = grad
        part[c, 0, at] = out
        part[c, 1, at] = row_grad

    def sum_slot(d, t):
        return (N_DP + 1 - t) % N_DP if d == 0 else t - 1

    def sum_copy(c, d, a, h, t):
        rows = pl.ds(h * 16, 16)
        return pltpu.make_async_remote_copy(
            src_ref=part.at[c, a, sum_slot(d, t), rows],
            dst_ref=arrived.at[c, a, N_DP - t if d == 0 else t % HALF, rows],
            send_sem=rs_send.at[c, d, 2 * a + h, t - 1],
            recv_sem=rs_recv.at[c, d, 2 * a + h, t - 1],
            device_id=beside(c, d),
            device_id_type=MESH,
        )

    def gather_step(s, carry):
        @pl.when(s <= HALF)
        def _():
            for a, h, c, d in ORDER:
                gather_copy(c, d, a, h, s - 1).wait_recv()
                if d == a:
                    gather_copy(c, d, a, h, s).start()
                else:
                    @pl.when(s < HALF)
                    def _():
                        gather_copy(c, d, a, h, s).start()

        @pl.when(s == 2)
        def _():
            for load in loads[6:]:
                load.wait()

        c = s % 2
        base = s - 2 - c
        behind, ahead = pl.ds(HALF - 1 - base, 2), pl.ds(HALF + base, 2)

        def both(a):
            return jnp.concatenate(
                [gathered[c, a, behind].reshape(64, width), gathered[c, a, ahead].reshape(64, width)]
            )

        values = experts(c, both(0), both(1))
        keep(c, behind, values, 0)
        keep(c, ahead, values, 2)

        @pl.when(s >= HALF)
        def _():
            for a in range(2):
                for h in range(2):
                    sum_copy(c, 1 - a, a, h, 2).start()

        return carry

    lax.fori_loop(2, HALF + 2, gather_step, 0)
    for c in range(2):
        for a in range(2):
            for h in range(2):
                gather_copy(c, a, a, h, HALF).wait_recv()
        keep(c, pl.ds(0, 1), experts(c, gathered[c, 0, 0], gathered[c, 1, 0]), 0)
        for a in range(2):
            for h in range(2):
                sum_copy(c, a, a, h, 1).start()

    def add(c, d, a, h, t):
        sum_copy(c, d, a, h, t - 1).wait_recv()
        at = (c, a, sum_slot(d, t), pl.ds(h * 16, 16))
        part[at] = (part[at].astype(F32) + arrived[at].astype(F32)).astype(BF16)
        sum_copy(c, d, a, h, t).start()

    def sent(s):
        for a, h, c, d in ORDER:
            if d == a:
                gather_copy(c, d, a, h, s).wait_send()
                sum_copy(c, d, a, h, s).wait_send()
            else:
                @pl.when(s < HALF)
                def _():
                    gather_copy(c, d, a, h, s).wait_send()
                    sum_copy(c, d, a, h, s + 1).wait_send()

    def sum_step(t, carry):
        for array in range(2):
            for a, h, c, d in ORDER:
                if a == array and d != a:
                    @pl.when(t < HALF)
                    def _():
                        add(c, d, a, h, t + 1)

            for a, h, c, d in ORDER:
                if a == array and d == a:
                    add(c, d, a, h, t)

        @pl.when(t <= width // 128 + 1)
        def _():
            part_of = pl.ds(pl.multiple_of((t - 2) * 128, 128), 128)
            for c in range(2):
                w_in_grad[c, part_of, :] = dot(
                    gathered[c, 0, :, :, part_of].reshape(1024, 128), pre_grad[c].reshape(1024, -1), 0, 0
                )
                w_out_grad[c, :, part_of] = dot(
                    hidden[c].reshape(1024, -1), gathered[c, 1, :, :, part_of].reshape(1024, 128), 0, 0
                )

        sent(t - 1)
        return carry

    lax.fori_loop(2, HALF + 1, sum_step, 0)
    home = (ret_send, ret_recv)
    for a in range(2):
        total = []
        for c in range(2):
            for d in range(2):
                for h in range(2):
                    sum_copy(c, d, a, h, HALF).wait_recv()
            at = part[c, a, HALF].astype(F32) + arrived[c, a, HALF].astype(F32)
            total.append((at + arrived[c, a, 0].astype(F32)).astype(BF16))
        total = jnp.concatenate(cut(jnp.concatenate(total)))
        send[a] = dot(unshuffle, total, 1, 0).astype(BF16).reshape(N_EXP, 16, left)
        exchange_start(send, back, a, home)
    sent(HALF)

    spans = (pl.ds(0, left), pl.ds(left, width - left))
    exchange_wait(send, back, 0, home)
    returned = back[0].reshape(128, left)
    inner = [0.0, 0.0]
    for h in range(2):
        picked = [dot(take[k][h], returned[:, : spans[h].size], 1, 0) for k in range(2)]
        mixed[:, spans[h]] = (gate[0] * picked[0] + gate[1] * picked[1]).astype(BF16)
        grad_wide = out_grad[:, spans[h]].astype(F32)
        for k in range(2):
            inner[k] += jnp.sum(picked[k] * grad_wide, axis=1, keepdims=True)
    for k in range(2):
        gate_grad[k : k + 1, :] = jnp.broadcast_to(inner[k], (128, 128)).T[:1]
    exchange_wait(send, back, 1, home)
    returned = back[1].reshape(128, left)
    for h in range(2):
        tok_grad[:, spans[h]] = dot(take_either[h], returned[:, : spans[h].size], 1, 0).astype(BF16)


def write_back(*refs):
    sems = refs[-1]
    copies = []
    for i in (3, 4, 0, 1, 2):
        source, target = refs[i], refs[5 + i]
        if len(source.shape) == 3:
            copies += [pltpu.make_async_copy(source.at[c], target.at[c], sems.at[i, c]) for c in range(2)]
        else:
            copies.append(pltpu.make_async_copy(source, target, sems.at[i, 0]))
    for copy in copies:
        copy.start()
    for copy in copies:
        copy.wait()


def per_device(tokens, expert_ids, slot_ids, dropped, gates, w_in, w_out, out_grad):
    count, width = tokens.shape
    hidden_units = w_in.shape[2]
    anywhere = pl.BlockSpec(memory_space=pl.ANY)
    blocks = pltpu.VMEM((2, 2, N_DP, 32, width), BF16)
    units = pltpu.VMEM((2, N_DP, 32, hidden_units), BF16)
    small = pltpu.VMEM((2, N_EXP, 16, (width // 128 + 1) // 2 * 128), BF16)
    dma = pltpu.SemaphoreType.DMA
    results = pl.pallas_call(
        kernel,
        out_shape=(
            pltpu.VMEM((count, width), BF16),
            pltpu.VMEM((count, width), BF16),
            pltpu.VMEM((2, count), F32),
            pltpu.VMEM(w_in.shape, F32),
            pltpu.VMEM(w_out.shape, F32),
        ),
        in_specs=[anywhere] * 8,
        scratch_shapes=[
            pltpu.VMEM((count, width), BF16),
            *[pltpu.VMEM((2, count), jnp.int32)] * 3,
            pltpu.VMEM((2, count), F32),
            pltpu.VMEM((count, width), BF16),
            pltpu.VMEM(w_in.shape, BF16), pltpu.VMEM(w_out.shape, BF16),
            blocks, blocks, blocks, units, units, small, small, small,
            dma((8,)), dma((2, N_EXP)), dma((2, N_EXP)),
            *[dma((2, 2, 4, HALF))] * 4,
            dma((2, N_EXP)), dma((2, N_EXP)),
        ],
        compiler_params=pltpu.CompilerParams(
            collective_id=0, has_side_effects=True, vmem_limit_bytes=50 * 1024 * 1024
        ),
        cost_estimate=pl.CostEstimate(
            flops=12 * 2048 * width * hidden_units, bytes_accessed=20_000_000, transcendentals=2_000_000
        ),
    )(tokens, expert_ids.T, slot_ids.T, dropped.T, gates.T, out_grad, w_in, w_out)
    mixed, tok_grad, gate_grad, w_in_grad, w_out_grad = pl.pallas_call(
        write_back,
        out_shape=[jax.ShapeDtypeStruct(v.shape, v.dtype) for v in results],
        in_specs=[anywhere] * 5,
        out_specs=[anywhere] * 5,
        scratch_shapes=[dma((5, 2))],
        compiler_params=pltpu.CompilerParams(vmem_limit_bytes=1024 * 1024),
    )(*results)
    return mixed, tok_grad, gate_grad.T, w_in_grad, w_out_grad


def solution(mesh):
    rows = P(("expert", "dp"), None)
    placed = (rows, rows, rows, rows, rows, P("expert", None, "dp"), P("expert", "dp", None), rows)
    return jax.shard_map(
        per_device,
        mesh=mesh,
        in_specs=placed,
        out_specs=(rows, rows, rows, P("expert", None, "dp"), P("expert", "dp", None)),
        check_vma=False,
    )
```

```python
import jax
import jax.numpy as jnp
from jax import lax
from jax.experimental import pallas as pl
from jax.experimental.pallas import tpu as pltpu
from jax.sharding import PartitionSpec as P

CAP = 4
N_EXP = 8
N_DP = 32
HALF = 16
TURNS = 8
BF16 = jnp.bfloat16
F32 = jnp.float32
MESH = pl.DeviceIdType.MESH
ORDER = [(a, h, c, d) for a in range(2) for h in range(2) for c in range(2) for d in range(2)]

inv_root_two = 0.7071067811865476
inv_root_two_pi = 0.3989422804014327


def place_first(y, z):
    return 4 * z + (y + z) % 4


def device_first(p):
    z = p // 4
    return ((p % 4 + 8 - z) % 4) * 8 + z


def place_second(y, z):
    w = (z + 24 - 3 * y) % 8
    return 4 * y + 16 * (w // 4) + w % 4


def device_second(p):
    q = p // 4
    return (q % 4) * 8 + (3 * q + p % 4) % 8


def dot(left, right, left_dim, right_dim):
    return lax.dot_general(
        left, right, (((left_dim,), (right_dim,)), ((), ())), preferred_element_type=F32
    )


def kernel(
    tokens_in, ids_in, slots_in, dropped_in, gates_in, out_grad_in, w_in_in, w_out_in,
    mixed, tok_grad, gate_grad, w_in_grad, w_out_grad,
    tokens, ids, slots, dropped, gates, out_grad, w_in, w_out,
    gathered, part, arrived, hidden, pre_grad, send, recv, back,
    load_sem, a2a_send, a2a_recv, ret_recv, ring_send, ring_recv,
):
    width = tokens.shape[1]
    left = send.shape[3]
    me_e = lax.axis_index("expert")
    me_d = lax.axis_index("dp")
    y, z = me_d // 8, me_d % 8
    here = (place_first(y, z), place_second(y, z))
    device = (device_first, device_second)
    near = [[device[c]((here[c] + step) % N_DP) for step in (1, N_DP - 1)] for c in range(2)]

    def beside(c, d):
        return {"dp": near[0][d] + c * (near[1][d] - near[0][d])}

    barrier = pltpu.get_barrier_semaphore()

    def greet(k, carry):
        pl.semaphore_signal(
            barrier, inc=1, device_id={"expert": (me_e + k) % N_EXP}, device_id_type=MESH
        )
        return carry

    lax.fori_loop(1, N_EXP, greet, 0)
    for c in range(2):
        for d in range(2):
            pl.semaphore_signal(barrier, inc=1, device_id={"dp": near[c][d]}, device_id_type=MESH)

    loads = [
        pltpu.make_async_copy(source, target, load_sem.at[i])
        for i, (source, target) in enumerate(
            (
                (ids_in, ids), (slots_in, slots), (dropped_in, dropped), (tokens_in, tokens),
                (gates_in, gates), (out_grad_in, out_grad), (w_in_in, w_in), (w_out_in, w_out),
            )
        )
    ]
    for load in loads:
        load.start()
    for load in loads[:4]:
        load.wait()

    expert = ids[...]
    column = (expert >> 1) * 16 + (expert & 1) * 4 + slots[...]
    column = jnp.where(dropped[...] == 0, column, -64)
    row = lax.broadcasted_iota(jnp.int32, (128, 128), 0)
    lane = lax.broadcasted_iota(jnp.int32, (128, 128), 1)

    def onehot(mask):
        return jnp.where(mask, 1.0, 0.0).astype(BF16)

    def cut(value):
        zeros = jnp.zeros((value.shape[0], 2 * left - width), BF16)
        return [value[:, :left], jnp.concatenate([value[:, left:], zeros], axis=1)]

    chosen = [[column[k : k + 1, :] + 8 * h == row for h in range(2)] for k in range(2)]
    either = [chosen[0][h] | chosen[1][h] for h in range(2)]

    def pack(a, masks, values):
        masks = jnp.concatenate([onehot(mask) for mask in masks], axis=1)
        send[a] = dot(masks, jnp.concatenate(values), 1, 0).astype(BF16).reshape(N_EXP, 16, left)

    def across(source, target, a, k, sems):
        return pltpu.make_async_remote_copy(
            src_ref=source.at[a, (me_e + k) % N_EXP],
            dst_ref=target.at[a, me_e],
            send_sem=sems[0].at[a, k],
            recv_sem=sems[1].at[a, k],
            device_id={"expert": (me_e + k) % N_EXP},
            device_id_type=MESH,
        )

    far_first = (4, 3, 5, 2, 6, 1, 7)

    def exchange_start(source, target, a, sems):
        for k in far_first:
            across(source, target, a, k, sems).start()
        target[a, me_e] = source[a, me_e]

    def exchange_wait(source, target, a, sems):
        for k in reversed(far_first):
            across(source, target, a, k, sems).wait()

    out_way = (a2a_send, a2a_recv)
    pack(0, either, cut(tokens[...]))
    pl.semaphore_wait(barrier, N_EXP + 3)
    exchange_start(send, recv, 0, out_way)
    for load in loads[4:6]:
        load.wait()
    gate = [jnp.broadcast_to(gates[k : k + 1, :], (128, 128)).T[:, :1] for k in range(2)]
    scaled = [cut((gate[k] * out_grad[...].astype(F32)).astype(BF16)) for k in range(2)]
    pack(1, chosen[0] + chosen[1], scaled[0] + scaled[1])
    exchange_start(send, recv, 1, out_way)

    out_row = row[:64]
    source_row = ((out_row & 31) >> 2) * 16 + (out_row >> 5) * 4 + (out_row & 3)
    shuffle = [onehot(source_row + 8 * h == lane[:64]) for h in range(2)]

    def gather_copy(c, d, a, h, s):
        rows = pl.ds(h * 16, 16)
        return pltpu.make_async_remote_copy(
            src_ref=gathered.at[c, a, HALF + 1 - s if d == 0 else HALF - 1 + s, rows],
            dst_ref=gathered.at[c, a, HALF - s if d == 0 else (HALF + s) % N_DP, rows],
            send_sem=ring_send.at[c, d, 2 * a + h, s % 2],
            recv_sem=ring_recv.at[c, d, 2 * a + h, s % TURNS],
            device_id=beside(c, d),
            device_id_type=MESH,
        )

    for a in range(2):
        exchange_wait(send, recv, a, out_way)
        got = recv[a].reshape(128, left)
        for h in range(2):
            block = dot(shuffle[h], got, 1, 0).astype(BF16)
            for c in range(2):
                if h == 0:
                    gathered[c, a, HALF, :, :left] = block[c * 32 : (c + 1) * 32]
                else:
                    gathered[c, a, HALF, :, left:] = block[c * 32 : (c + 1) * 32, : width - left]
        for h in range(2):
            for c in range(2):
                for d in range(2):
                    gather_copy(c, d, a, h, 1).start()

    def turned(mask):
        return jnp.where(mask, 1.0, 0.0).T.astype(BF16)

    take = [[turned(chosen[k][h]) for h in range(2)] for k in range(2)]
    take_either = [turned(either[h]) for h in range(2)]
    block_row = lane & 63
    back_row = ((block_row & 31) >> 2) * 16 + (block_row >> 5) * 4 + (block_row & 3) + (lane >> 6) * 8
    unshuffle = onehot(back_row == row)

    def experts(c, rows, grads):
        count = rows.shape[0]
        pre = dot(rows, w_in[c], 1, 0)
        erf = 1.0 + lax.erf(pre * inv_root_two)
        hid = (0.5 * pre * erf).astype(BF16)
        slope = 0.5 * erf + pre * jnp.exp(-0.5 * pre * pre) * inv_root_two_pi
        grad = (dot(grads, w_out[c], 1, 1) * slope).astype(BF16)
        out = dot(hid, w_out[c], 1, 0).astype(BF16)
        row_grad = dot(grad, w_in[c], 1, 1).astype(BF16)
        shape = (count // 32, 32, -1)
        return [v.reshape(shape) for v in (hid, grad, out, row_grad)]

    def keep(c, at, values, first):
        hid, grad, out, row_grad = (v[first : first + at.size] for v in values)
        hidden[c, at] = hid
        pre_grad[c, at] = grad
        part[c, 0, at] = out
        part[c, 1, at] = row_grad

    def sum_slot(d, t):
        return (N_DP + 1 - t) % N_DP if d == 0 else t - 1

    def sum_copy(c, d, a, h, t):
        rows = pl.ds(h * 16, 16)
        return pltpu.make_async_remote_copy(
            src_ref=part.at[c, a, sum_slot(d, t), rows],
            dst_ref=arrived.at[c, a, N_DP - t if d == 0 else t % HALF, rows],
            send_sem=ring_send.at[c, d, 2 * a + h, t % 2],
            recv_sem=ring_recv.at[c, d, 2 * a + h, t % TURNS],
            device_id=beside(c, d),
            device_id_type=MESH,
        )

    def after_last(copy):
        copy.wait_send()
        copy.start()

    def gather_step(s, carry):
        @pl.when(s <= HALF)
        def _():
            for a, h, c, d in ORDER:
                gather_copy(c, d, a, h, s - 1).wait_recv()

                @pl.when(s > 2)
                def _():
                    if d == a:
                        after_last(gather_copy(c, d, a, h, s))
                    else:
                        pl.when(s < HALF)(lambda: after_last(gather_copy(c, d, a, h, s)))

                @pl.when(s == 2)
                def _():
                    gather_copy(c, d, a, h, s).start()

        @pl.when(s == 2)
        def _():
            for load in loads[6:]:
                load.wait()

        c = s % 2
        base = s - 2 - c
        behind, ahead = pl.ds(HALF - 1 - base, 2), pl.ds(HALF + base, 2)

        def both(a):
            return jnp.concatenate(
                [gathered[c, a, behind].reshape(64, width), gathered[c, a, ahead].reshape(64, width)]
            )

        values = experts(c, both(0), both(1))
        keep(c, behind, values, 0)
        keep(c, ahead, values, 2)

        @pl.when(s >= HALF)
        def _():
            for a in range(2):
                for h in range(2):
                    after_last(sum_copy(c, 1 - a, a, h, 2))

        return carry

    lax.fori_loop(2, HALF + 2, gather_step, 0)
    for c in range(2):
        for a in range(2):
            for h in range(2):
                gather_copy(c, a, a, h, HALF).wait_recv()
        keep(c, pl.ds(0, 1), experts(c, gathered[c, 0, 0], gathered[c, 1, 0]), 0)
        for a in range(2):
            for h in range(2):
                after_last(sum_copy(c, a, a, h, 1))

    def add(c, d, a, h, t):
        sum_copy(c, d, a, h, t - 1).wait_recv()
        at = (c, a, sum_slot(d, t), pl.ds(h * 16, 16))
        part[at] = (part[at].astype(F32) + arrived[at].astype(F32)).astype(BF16)
        after_last(sum_copy(c, d, a, h, t))

    def sum_step(t, carry):
        for array in range(2):
            for a, h, c, d in ORDER:
                if a == array and d != a:
                    @pl.when(t < HALF)
                    def _():
                        add(c, d, a, h, t + 1)

            for a, h, c, d in ORDER:
                if a == array and d == a:
                    add(c, d, a, h, t)

        @pl.when(t <= width // 128 + 1)
        def _():
            part_of = pl.ds(pl.multiple_of((t - 2) * 128, 128), 128)
            for c in range(2):
                w_in_grad[c, part_of, :] = dot(
                    gathered[c, 0, :, :, part_of].reshape(1024, 128), pre_grad[c].reshape(1024, -1), 0, 0
                )
                w_out_grad[c, :, part_of] = dot(
                    hidden[c].reshape(1024, -1), gathered[c, 1, :, :, part_of].reshape(1024, 128), 0, 0
                )

        return carry

    lax.fori_loop(2, HALF + 1, sum_step, 0)
    home = (a2a_send, ret_recv)
    for a in range(2):
        total = []
        for c in range(2):
            for d in range(2):
                for h in range(2):
                    sum_copy(c, d, a, h, HALF).wait_recv()
            at = part[c, a, HALF].astype(F32) + arrived[c, a, HALF].astype(F32)
            total.append((at + arrived[c, a, 0].astype(F32)).astype(BF16))
        total = jnp.concatenate(cut(jnp.concatenate(total)))
        send[a] = dot(unshuffle, total, 1, 0).astype(BF16).reshape(N_EXP, 16, left)
        exchange_start(send, back, a, home)
    for a, h, c, d in ORDER:
        for t in (HALF - 1, HALF):
            sum_copy(c, d, a, h, t).wait_send()

    spans = (pl.ds(0, left), pl.ds(left, width - left))
    exchange_wait(send, back, 0, home)
    returned = back[0].reshape(128, left)
    inner = [0.0, 0.0]
    for h in range(2):
        picked = [dot(take[k][h], returned[:, : spans[h].size], 1, 0) for k in range(2)]
        mixed[:, spans[h]] = (gate[0] * picked[0] + gate[1] * picked[1]).astype(BF16)
        grad_wide = out_grad[:, spans[h]].astype(F32)
        for k in range(2):
            inner[k] += jnp.sum(picked[k] * grad_wide, axis=1, keepdims=True)
    for k in range(2):
        gate_grad[k : k + 1, :] = jnp.broadcast_to(inner[k], (128, 128)).T[:1]
    exchange_wait(send, back, 1, home)
    returned = back[1].reshape(128, left)
    for h in range(2):
        tok_grad[:, spans[h]] = dot(take_either[h], returned[:, : spans[h].size], 1, 0).astype(BF16)


def write_back(*refs):
    sems = refs[-1]
    copies = []
    for i in (3, 4, 0, 1, 2):
        source, target = refs[i], refs[5 + i]
        if len(source.shape) == 3:
            copies += [pltpu.make_async_copy(source.at[c], target.at[c], sems.at[i, c]) for c in range(2)]
        else:
            copies.append(pltpu.make_async_copy(source, target, sems.at[i, 0]))
    for copy in copies:
        copy.start()
    for copy in copies:
        copy.wait()


def per_device(tokens, expert_ids, slot_ids, dropped, gates, w_in, w_out, out_grad):
    count, width = tokens.shape
    hidden_units = w_in.shape[2]
    anywhere = pl.BlockSpec(memory_space=pl.ANY)
    blocks = pltpu.VMEM((2, 2, N_DP, 32, width), BF16)
    units = pltpu.VMEM((2, N_DP, 32, hidden_units), BF16)
    small = pltpu.VMEM((2, N_EXP, 16, (width // 128 + 1) // 2 * 128), BF16)
    dma = pltpu.SemaphoreType.DMA
    results = pl.pallas_call(
        kernel,
        out_shape=(
            pltpu.VMEM((count, width), BF16),
            pltpu.VMEM((count, width), BF16),
            pltpu.VMEM((2, count), F32),
            pltpu.VMEM(w_in.shape, F32),
            pltpu.VMEM(w_out.shape, F32),
        ),
        in_specs=[anywhere] * 8,
        scratch_shapes=[
            pltpu.VMEM((count, width), BF16),
            *[pltpu.VMEM((2, count), jnp.int32)] * 3,
            pltpu.VMEM((2, count), F32),
            pltpu.VMEM((count, width), BF16),
            pltpu.VMEM(w_in.shape, BF16), pltpu.VMEM(w_out.shape, BF16),
            blocks, blocks, blocks, units, units, small, small, small,
            dma((8,)), dma((2, N_EXP)), dma((2, N_EXP)), dma((2, N_EXP)),
            dma((2, 2, 4, 2)), dma((2, 2, 4, TURNS)),
        ],
        compiler_params=pltpu.CompilerParams(
            collective_id=0, has_side_effects=True, vmem_limit_bytes=50 * 1024 * 1024
        ),
        cost_estimate=pl.CostEstimate(
            flops=12 * 2048 * width * hidden_units, bytes_accessed=20_000_000, transcendentals=2_000_000
        ),
    )(tokens, expert_ids.T, slot_ids.T, dropped.T, gates.T, out_grad, w_in, w_out)
    mixed, tok_grad, gate_grad, w_in_grad, w_out_grad = pl.pallas_call(
        write_back,
        out_shape=[jax.ShapeDtypeStruct(v.shape, v.dtype) for v in results],
        in_specs=[anywhere] * 5,
        out_specs=[anywhere] * 5,
        scratch_shapes=[dma((5, 2))],
        compiler_params=pltpu.CompilerParams(vmem_limit_bytes=1024 * 1024),
    )(*results)
    return mixed, tok_grad, gate_grad.T, w_in_grad, w_out_grad


def solution(mesh):
    rows = P(("expert", "dp"), None)
    placed = (rows, rows, rows, rows, rows, P("expert", None, "dp"), P("expert", "dp", None), rows)
    return jax.shard_map(
        per_device,
        mesh=mesh,
        in_specs=placed,
        out_specs=(rows, rows, rows, P("expert", None, "dp"), P("expert", "dp", None)),
        check_vma=False,
    )
```

```python
import jax
import jax.numpy as jnp
from jax import lax
from jax.experimental import pallas as pl
from jax.experimental.pallas import tpu as pltpu
from jax.sharding import PartitionSpec as P

CAP = 4
N_EXP = 8
N_DP = 32
HALF = 16
TURNS = 8
BF16 = jnp.bfloat16
F32 = jnp.float32
MESH = pl.DeviceIdType.MESH
ORDER = [(a, h, c, d) for a in range(2) for h in range(2) for c in range(2) for d in range(2)]

inv_root_two = 0.7071067811865476
inv_root_two_pi = 0.3989422804014327


def place_first(y, z):
    return 4 * z + (y + z) % 4


def device_first(p):
    z = p // 4
    return ((p % 4 + 8 - z) % 4) * 8 + z


def place_second(y, z):
    w = (z + 24 - 3 * y) % 8
    return 4 * y + 16 * (w // 4) + w % 4


def device_second(p):
    q = p // 4
    return (q % 4) * 8 + (3 * q + p % 4) % 8


def dot(left, right, left_dim, right_dim):
    return lax.dot_general(
        left, right, (((left_dim,), (right_dim,)), ((), ())), preferred_element_type=F32
    )


def kernel(
    tokens_in, ids_in, slots_in, dropped_in, gates_in, out_grad_in, w_in_in, w_out_in,
    mixed, tok_grad, gate_grad, w_in_grad, w_out_grad,
    tokens, ids, slots, dropped, gates, out_grad, w_in, w_out,
    gathered, part, arrived, hidden, pre_grad, send, recv, back,
    load_sem, a2a_send, a2a_recv, ret_recv, ring_send, ring_recv,
):
    width = tokens.shape[1]
    left = send.shape[3]
    me_e = lax.axis_index("expert")
    me_d = lax.axis_index("dp")
    y, z = me_d // 8, me_d % 8
    here = (place_first(y, z), place_second(y, z))
    device = (device_first, device_second)
    near = [[device[c]((here[c] + step) % N_DP) for step in (1, N_DP - 1)] for c in range(2)]

    def beside(c, d):
        return {"dp": near[0][d] + c * (near[1][d] - near[0][d])}

    barrier = pltpu.get_barrier_semaphore()

    def greet(k, carry):
        pl.semaphore_signal(
            barrier, inc=1, device_id={"expert": (me_e + k) % N_EXP}, device_id_type=MESH
        )
        return carry

    lax.fori_loop(1, N_EXP, greet, 0)
    for c in range(2):
        for d in range(2):
            pl.semaphore_signal(barrier, inc=1, device_id={"dp": near[c][d]}, device_id_type=MESH)

    loads = [
        pltpu.make_async_copy(source, target, load_sem.at[i])
        for i, (source, target) in enumerate(
            (
                (ids_in, ids), (slots_in, slots), (dropped_in, dropped), (tokens_in, tokens),
                (gates_in, gates), (out_grad_in, out_grad), (w_in_in, w_in), (w_out_in, w_out),
            )
        )
    ]
    for load in loads:
        load.start()
    for load in loads[:4]:
        load.wait()

    expert = ids[...]
    column = (expert >> 1) * 16 + (expert & 1) * 4 + slots[...]
    column = jnp.where(dropped[...] == 0, column, -64)
    row = lax.broadcasted_iota(jnp.int32, (128, 128), 0)
    lane = lax.broadcasted_iota(jnp.int32, (128, 128), 1)

    def onehot(mask):
        return jnp.where(mask, 1.0, 0.0).astype(BF16)

    def cut(value):
        zeros = jnp.zeros((value.shape[0], 2 * left - width), BF16)
        return [value[:, :left], jnp.concatenate([value[:, left:], zeros], axis=1)]

    chosen = [[column[k : k + 1, :] + 8 * h == row for h in range(2)] for k in range(2)]
    either = [chosen[0][h] | chosen[1][h] for h in range(2)]

    def pack(a, masks, values):
        masks = jnp.concatenate([onehot(mask) for mask in masks], axis=1)
        send[a] = dot(masks, jnp.concatenate(values), 1, 0).astype(BF16).reshape(N_EXP, 16, left)

    def across(source, target, a, k, sems):
        return pltpu.make_async_remote_copy(
            src_ref=source.at[a, (me_e + k) % N_EXP],
            dst_ref=target.at[a, me_e],
            send_sem=sems[0].at[a, k],
            recv_sem=sems[1].at[a, k],
            device_id={"expert": (me_e + k) % N_EXP},
            device_id_type=MESH,
        )

    far_first = (4, 3, 5, 2, 6, 1, 7)

    def exchange_start(source, target, a, sems):
        for k in far_first:
            across(source, target, a, k, sems).start()
        target[a, me_e] = source[a, me_e]

    def exchange_wait(source, target, a, sems):
        for k in reversed(far_first):
            across(source, target, a, k, sems).wait()

    out_way = (a2a_send, a2a_recv)
    pack(0, either, cut(tokens[...]))
    pl.semaphore_wait(barrier, N_EXP + 3)
    exchange_start(send, recv, 0, out_way)
    for load in loads[4:6]:
        load.wait()
    gate = [jnp.broadcast_to(gates[k : k + 1, :], (128, 128)).T[:, :1] for k in range(2)]
    scaled = [cut((gate[k] * out_grad[...].astype(F32)).astype(BF16)) for k in range(2)]
    pack(1, chosen[0] + chosen[1], scaled[0] + scaled[1])
    exchange_start(send, recv, 1, out_way)

    out_row = row[:64]
    source_row = ((out_row & 31) >> 2) * 16 + (out_row >> 5) * 4 + (out_row & 3)
    shuffle = [onehot(source_row + 8 * h == lane[:64]) for h in range(2)]

    def gather_copy(c, d, a, h, s):
        rows = pl.ds(h * 16, 16)
        return pltpu.make_async_remote_copy(
            src_ref=gathered.at[c, a, HALF + 1 - s if d == 0 else HALF - 1 + s, rows],
            dst_ref=gathered.at[c, a, HALF - s if d == 0 else (HALF + s) % N_DP, rows],
            send_sem=ring_send.at[c, d, 2 * a + h, s % 2],
            recv_sem=ring_recv.at[c, d, 2 * a + h, s % TURNS],
            device_id=beside(c, d),
            device_id_type=MESH,
        )

    for a in range(2):
        exchange_wait(send, recv, a, out_way)
        got = recv[a].reshape(128, left)
        for h in range(2):
            block = dot(shuffle[h], got, 1, 0).astype(BF16)
            for c in range(2):
                if h == 0:
                    gathered[c, a, HALF, :, :left] = block[c * 32 : (c + 1) * 32]
                else:
                    gathered[c, a, HALF, :, left:] = block[c * 32 : (c + 1) * 32, : width - left]
        for h in range(2):
            for c in range(2):
                for d in range(2):
                    gather_copy(c, d, a, h, 1).start()

    def turned(mask):
        return jnp.where(mask, 1.0, 0.0).T.astype(BF16)

    take = [[turned(chosen[k][h]) for h in range(2)] for k in range(2)]
    take_either = [turned(either[h]) for h in range(2)]
    block_row = lane & 63
    back_row = ((block_row & 31) >> 2) * 16 + (block_row >> 5) * 4 + (block_row & 3) + (lane >> 6) * 8
    unshuffle = onehot(back_row == row)

    def experts(c, rows, grads):
        count = rows.shape[0]
        pre = dot(rows, w_in[c], 1, 0)
        erf = 1.0 + lax.erf(pre * inv_root_two)
        hid = (0.5 * pre * erf).astype(BF16)
        slope = 0.5 * erf + pre * jnp.exp(-0.5 * pre * pre) * inv_root_two_pi
        grad = (dot(grads, w_out[c], 1, 1) * slope).astype(BF16)
        out = dot(hid, w_out[c], 1, 0).astype(BF16)
        row_grad = dot(grad, w_in[c], 1, 1).astype(BF16)
        shape = (count // 32, 32, -1)
        return [v.reshape(shape) for v in (hid, grad, out, row_grad)]

    def keep(c, at, values, first):
        hid, grad, out, row_grad = (v[first : first + at.size] for v in values)
        hidden[c, at] = hid
        pre_grad[c, at] = grad
        part[c, 0, at] = out
        part[c, 1, at] = row_grad

    def sum_slot(d, t):
        return (N_DP + 1 - t) % N_DP if d == 0 else t - 1

    def sum_copy(c, d, a, h, t):
        rows = pl.ds(h * 16, 16)
        return pltpu.make_async_remote_copy(
            src_ref=part.at[c, a, sum_slot(d, t), rows],
            dst_ref=arrived.at[c, a, N_DP - t if d == 0 else t % HALF, rows],
            send_sem=ring_send.at[c, d, 2 * a + h, t % 2],
            recv_sem=ring_recv.at[c, d, 2 * a + h, t % TURNS],
            device_id=beside(c, d),
            device_id_type=MESH,
        )

    def after_last(copy):
        copy.wait_send()
        copy.start()

    def gather_step(s, carry):
        @pl.when(s <= HALF)
        def _():
            for a, h, c, d in ORDER:
                gather_copy(c, d, a, h, s - 1).wait_recv()

                @pl.when(s > 2)
                def _():
                    if d == h:
                        after_last(gather_copy(c, d, a, h, s))
                    else:
                        pl.when(s < HALF)(lambda: after_last(gather_copy(c, d, a, h, s)))

                @pl.when(s == 2)
                def _():
                    gather_copy(c, d, a, h, s).start()

        @pl.when(s == 2)
        def _():
            for load in loads[6:]:
                load.wait()

        c = s % 2
        base = s - 2 - c
        behind, ahead = pl.ds(HALF - 1 - base, 2), pl.ds(HALF + base, 2)

        def both(a):
            return jnp.concatenate(
                [gathered[c, a, behind].reshape(64, width), gathered[c, a, ahead].reshape(64, width)]
            )

        values = experts(c, both(0), both(1))
        keep(c, behind, values, 0)
        keep(c, ahead, values, 2)

        @pl.when(s >= HALF)
        def _():
            for a in range(2):
                for h in range(2):
                    after_last(sum_copy(c, 1 - h, a, h, 2))

        return carry

    lax.fori_loop(2, HALF + 2, gather_step, 0)
    for c in range(2):
        for a in range(2):
            for h in range(2):
                gather_copy(c, h, a, h, HALF).wait_recv()
        keep(c, pl.ds(0, 1), experts(c, gathered[c, 0, 0], gathered[c, 1, 0]), 0)
        for a in range(2):
            for h in range(2):
                after_last(sum_copy(c, h, a, h, 1))

    def add(c, d, a, h, t):
        sum_copy(c, d, a, h, t - 1).wait_recv()
        at = (c, a, sum_slot(d, t), pl.ds(h * 16, 16))
        part[at] = (part[at].astype(F32) + arrived[at].astype(F32)).astype(BF16)
        after_last(sum_copy(c, d, a, h, t))

    def sum_step(t, carry):
        for array in range(2):
            for a, h, c, d in ORDER:
                if a == array and d != h:
                    @pl.when(t < HALF)
                    def _():
                        add(c, d, a, h, t + 1)

            for a, h, c, d in ORDER:
                if a == array and d == h:
                    add(c, d, a, h, t)

        @pl.when(t <= width // 128 + 1)
        def _():
            part_of = pl.ds(pl.multiple_of((t - 2) * 128, 128), 128)
            for c in range(2):
                w_in_grad[c, part_of, :] = dot(
                    gathered[c, 0, :, :, part_of].reshape(1024, 128), pre_grad[c].reshape(1024, -1), 0, 0
                )
                w_out_grad[c, :, part_of] = dot(
                    hidden[c].reshape(1024, -1), gathered[c, 1, :, :, part_of].reshape(1024, 128), 0, 0
                )

        return carry

    lax.fori_loop(2, HALF + 1, sum_step, 0)
    home = (a2a_send, ret_recv)
    for a in range(2):
        total = []
        for c in range(2):
            for d in range(2):
                for h in range(2):
                    sum_copy(c, d, a, h, HALF).wait_recv()
            at = part[c, a, HALF].astype(F32) + arrived[c, a, HALF].astype(F32)
            total.append((at + arrived[c, a, 0].astype(F32)).astype(BF16))
        total = jnp.concatenate(cut(jnp.concatenate(total)))
        send[a] = dot(unshuffle, total, 1, 0).astype(BF16).reshape(N_EXP, 16, left)
        exchange_start(send, back, a, home)
    for a, h, c, d in ORDER:
        for t in (HALF - 1, HALF):
            sum_copy(c, d, a, h, t).wait_send()

    spans = (pl.ds(0, left), pl.ds(left, width - left))
    exchange_wait(send, back, 0, home)
    returned = back[0].reshape(128, left)
    inner = [0.0, 0.0]
    for h in range(2):
        picked = [dot(take[k][h], returned[:, : spans[h].size], 1, 0) for k in range(2)]
        mixed[:, spans[h]] = (gate[0] * picked[0] + gate[1] * picked[1]).astype(BF16)
        grad_wide = out_grad[:, spans[h]].astype(F32)
        for k in range(2):
            inner[k] += jnp.sum(picked[k] * grad_wide, axis=1, keepdims=True)
    for k in range(2):
        gate_grad[k : k + 1, :] = jnp.broadcast_to(inner[k], (128, 128)).T[:1]
    exchange_wait(send, back, 1, home)
    returned = back[1].reshape(128, left)
    for h in range(2):
        tok_grad[:, spans[h]] = dot(take_either[h], returned[:, : spans[h].size], 1, 0).astype(BF16)


def write_back(*refs):
    sems = refs[-1]
    copies = []
    for i in (3, 4, 0, 1, 2):
        source, target = refs[i], refs[5 + i]
        if len(source.shape) == 3:
            size = source.shape[1] // 2
            for q in range(4):
                at = (q // 2, pl.ds(q % 2 * size, size))
                copies.append(pltpu.make_async_copy(source.at[at], target.at[at], sems.at[i, q]))
        else:
            copies.append(pltpu.make_async_copy(source, target, sems.at[i, 0]))
    for copy in copies:
        copy.start()
    for copy in copies:
        copy.wait()


def per_device(tokens, expert_ids, slot_ids, dropped, gates, w_in, w_out, out_grad):
    count, width = tokens.shape
    hidden_units = w_in.shape[2]
    anywhere = pl.BlockSpec(memory_space=pl.ANY)
    blocks = pltpu.VMEM((2, 2, N_DP, 32, width), BF16)
    units = pltpu.VMEM((2, N_DP, 32, hidden_units), BF16)
    small = pltpu.VMEM((2, N_EXP, 16, (width // 128 + 1) // 2 * 128), BF16)
    dma = pltpu.SemaphoreType.DMA
    results = pl.pallas_call(
        kernel,
        out_shape=(
            pltpu.VMEM((count, width), BF16),
            pltpu.VMEM((count, width), BF16),
            pltpu.VMEM((2, count), F32),
            pltpu.VMEM(w_in.shape, F32),
            pltpu.VMEM(w_out.shape, F32),
        ),
        in_specs=[anywhere] * 8,
        scratch_shapes=[
            pltpu.VMEM((count, width), BF16),
            *[pltpu.VMEM((2, count), jnp.int32)] * 3,
            pltpu.VMEM((2, count), F32),
            pltpu.VMEM((count, width), BF16),
            pltpu.VMEM(w_in.shape, BF16), pltpu.VMEM(w_out.shape, BF16),
            blocks, blocks, blocks, units, units, small, small, small,
            dma((8,)), dma((2, N_EXP)), dma((2, N_EXP)), dma((2, N_EXP)),
            dma((2, 2, 4, 2)), dma((2, 2, 4, TURNS)),
        ],
        compiler_params=pltpu.CompilerParams(
            collective_id=0, has_side_effects=True, vmem_limit_bytes=50 * 1024 * 1024
        ),
        cost_estimate=pl.CostEstimate(
            flops=12 * 2048 * width * hidden_units, bytes_accessed=20_000_000, transcendentals=2_000_000
        ),
    )(tokens, expert_ids.T, slot_ids.T, dropped.T, gates.T, out_grad, w_in, w_out)
    mixed, tok_grad, gate_grad, w_in_grad, w_out_grad = pl.pallas_call(
        write_back,
        out_shape=[jax.ShapeDtypeStruct(v.shape, v.dtype) for v in results],
        in_specs=[anywhere] * 5,
        out_specs=[anywhere] * 5,
        scratch_shapes=[dma((5, 4))],
        compiler_params=pltpu.CompilerParams(vmem_limit_bytes=1024 * 1024),
    )(*results)
    return mixed, tok_grad, gate_grad.T, w_in_grad, w_out_grad


def solution(mesh):
    rows = P(("expert", "dp"), None)
    placed = (rows, rows, rows, rows, rows, P("expert", None, "dp"), P("expert", "dp", None), rows)
    return jax.shard_map(
        per_device,
        mesh=mesh,
        in_specs=placed,
        out_specs=(rows, rows, rows, P("expert", None, "dp"), P("expert", "dp", None)),
        check_vma=False,
    )
```
